512 devices in a mesh: seq: 32 (over y, z_hi, core), row: 4 (over x), col: 4 (over z_lo).
Axes of the slice: x: 4, y: 8, z: 8 (z_hi: 2, z_lo: 4; z = z_hi * 4 + z_lo), core: 2. Of those that a mesh axis runs over, the one named last changes fastest.
Arguments:
- query_rows: bfloat16 [5120, 48, 128], P('seq', ('row', 'col')), may hold values from -6 to 6
- key_rows: bfloat16 [5120, 48, 128], P('seq', ('row', 'col')), may hold values from -6 to 6
- value_rows: bfloat16 [5120, 48, 128], P('seq', ('row', 'col')), may hold values from -6 to 6
- out_weight: bfloat16 [48, 128, 6144], P('row', 'seq', 'col'), may hold values from -0.3125 to 0.3125
- out_bias: float32 [6144], P('col'), may hold values from -3 to 3
Outputs:
- output: bfloat16 [5120, 6144], P(('seq', 'row'), 'col')
The draws below stay inside these ranges and needn't reach their ends.
All inputs are finite; a program needn't handle non-finite values.
Results may differ from the reference program's by a relative error of at most 0.015.
Values may be sent and summed in bfloat16 or wider, within the bound.
No kernel may reach another device: no remote copies, remote signals or barrier semaphores. Data moves between devices by JAX's collectives and lax.ppermute only.
A program may use at most 64 MiB of HBM per device.

```python
import jax
import jax.numpy as jnp
from jax import lax

HEADS = 48
DH = 128
DOUT = 6144
TOKENS = 5120


def draw_query_rows(key, part):
    key = jax.random.fold_in(key, 11)
    sampled = 1.4 * jax.random.truncated_normal(key, -4.0, 4.0, (TOKENS, HEADS, DH), jnp.float32)
    return sampled.astype(jnp.bfloat16)


def draw_key_rows(key, part):
    key = jax.random.fold_in(key, 23)
    sampled = 1.4 * jax.random.truncated_normal(key, -4.0, 4.0, (TOKENS, HEADS, DH), jnp.float32)
    return sampled.astype(jnp.bfloat16)


def level_of(own_key, extent, shards, smallest, largest):
    loudness, own = 1.0, jax.random.fold_in(own_key, 6)
    for position, blocks in shards:
        steps = jnp.exp(jax.random.uniform(jax.random.fold_in(own, position), (blocks,), jnp.float32, smallest / len(shards), largest / len(shards)))
        loudness = loudness * jnp.repeat(steps, extent[position] // blocks).reshape([-1 if axis == position else 1 for axis in range(len(extent))])
    return loudness


def bell_draw(own_key, dims, scale, most, pieces=(), held_as=jnp.bfloat16):
    entries = scale * jax.random.normal(own_key, dims, jnp.float32)
    if pieces:
        entries = entries * level_of(own_key, dims, pieces, -0.22, 0.18)
    return jnp.clip(entries, -most, most).astype(held_as)


def setup_inputs(seed: int = 0) -> dict:
    keys = jax.random.split(jax.random.key(seed), 6)
    return {
        "query_rows": draw_query_rows(jax.random.fold_in(keys[5], 71), 0),
        "key_rows": draw_key_rows(jax.random.fold_in(keys[5], 71), 0),
        "value_rows": bell_draw(keys[2], (TOKENS, HEADS, DH), 1.0, 6.0, ((0, 32), (1, 16))),
        "out_weight": bell_draw(keys[3], (HEADS, DH, DOUT), (HEADS * DH // 16) ** -0.5, 0.3125, ((0, 4), (1, 32), (2, 4))),
        "out_bias": bell_draw(keys[4], (DOUT,), 0.5, 3.0, ((0, 4),), jnp.float32),
    }


def head_attention(arrays):
    head_query, head_key, head_value = arrays
    scores = jnp.dot(head_query, jnp.transpose(head_key), preferred_element_type=jnp.float32) * (DH ** -0.5)
    places = jnp.arange(TOKENS)
    allowed = places[None, :] <= places[:, None]
    scores = jnp.where(allowed, scores, -1e30)
    row_max = jnp.max(scores, axis=1, keepdims=True)
    attn_weights = jnp.where(allowed, jnp.exp(scores - row_max), 0.0)
    row_total = jnp.sum(attn_weights, axis=1, keepdims=True)
    weighted = jnp.dot(attn_weights.astype(jnp.bfloat16), head_value, preferred_element_type=jnp.float32)
    return (weighted / row_total).astype(jnp.bfloat16)


def reference(query_rows, key_rows, value_rows, out_weight, out_bias):
    stacked = lax.map(head_attention, (jnp.swapaxes(query_rows, 0, 1), jnp.swapaxes(key_rows, 0, 1), jnp.swapaxes(value_rows, 0, 1)))
    attended = jnp.swapaxes(stacked, 0, 1).reshape(TOKENS, HEADS * DH)
    projected = jnp.dot(attended, out_weight.reshape(HEADS * DH, DOUT), preferred_element_type=jnp.float32)
    return (projected + out_bias[None, :]).astype(jnp.bfloat16)
```

```python
import functools
import math

import jax
import jax.numpy as jnp
from jax import lax
from jax.experimental import pallas as pl
from jax.experimental.pallas import tpu as pltpu
from jax.sharding import Mesh
from jax.sharding import PartitionSpec as P

LOW = -1e30
VMEM = pl.BlockSpec(memory_space=pltpu.VMEM)
SMEM = pl.BlockSpec(memory_space=pltpu.SMEM)
PARAMS = pltpu.CompilerParams(vmem_limit_bytes=48 * 1024 * 1024)


def split3(x):
    high = x.astype(jnp.bfloat16).astype(jnp.float32)
    rest = x - high
    mid = rest.astype(jnp.bfloat16).astype(jnp.float32)
    return high, mid, rest - mid


def put_logs(logs, rows):
    lane = lax.broadcasted_iota(jnp.int32, (rows, 128), 1)
    plane = jnp.zeros((rows, 128), jnp.float32)
    for head, value in enumerate(logs):
        for part, piece in enumerate(split3(value)):
            plane = jnp.where(lane == 3 * head + part, piece, plane)
    return plane.astype(jnp.bfloat16)


def get_log(plane, head):
    wide = plane.astype(jnp.float32)
    at = 3 * head
    return wide[:, at : at + 1] + wide[:, at + 1 : at + 2] + wide[:, at + 2 : at + 3]


def attend_kernel(
    rows, heads, ring, scale2, idx_ref, qo_ref, qx_ref, own_ref, b1_ref, b2_ref, b3_ref, b4_ref,
    keep_ref, send_ref, m_ref, l_ref, acc_ref, log_ref,
):
    y, zh, c = idx_ref[0], idx_ref[1], idx_ref[2]
    all_rows = 4 * rows
    local = lax.broadcasted_iota(jnp.int32, (rows, 1), 0)
    query_pos = jnp.concatenate(
        [((zh if z == 0 else 1 - zh) * 2 + cc) * rows + local for z in range(2) for cc in range(2)], axis=0
    )
    key_pos = (zh * 2 + c) * rows + lax.broadcasted_iota(jnp.int32, (1, rows), 1)

    def step(h, query, keys, values, masked):
        scores = lax.dot_general(
            query, keys, (((1,), (1,)), ((), ())), preferred_element_type=jnp.float32
        )
        scores = scores * scale2
        if masked:
            scores = jnp.where(key_pos <= query_pos, scores, LOW)
        old = m_ref[...]
        new = jnp.maximum(old, jnp.max(scores, axis=1, keepdims=True))
        weights = jnp.exp2(scores - new)
        if masked:
            weights = jnp.where(key_pos <= query_pos, weights, 0.0)
        fade = jnp.exp2(old - new)
        m_ref[...] = new
        l_ref[...] = l_ref[...] * fade + jnp.sum(weights, axis=1, keepdims=True)
        acc_ref[...] = acc_ref[...] * fade + jnp.dot(
            weights.astype(jnp.bfloat16), values, preferred_element_type=jnp.float32
        )

    def head(h, carry):
        query = jnp.concatenate([qo_ref[0, h], qo_ref[1, h], qx_ref[0, h], qx_ref[1, h]], axis=0)
        m_ref[...] = jnp.full_like(m_ref, LOW)
        l_ref[...] = jnp.zeros_like(l_ref)
        acc_ref[...] = jnp.zeros_like(acc_ref)
        step(h, query, own_ref[0, h], own_ref[1, h], True)
        for distance, block in ((1, b1_ref), (2, b2_ref), (3, b3_ref), (4, b4_ref)):
            source = jnp.where(c == 0, y + ring - distance, y + distance) % ring

            @pl.when(source < y)
            def _():
                if distance < 4:
                    keys = jnp.concatenate([block[0, 0, h], block[1, 0, h]], axis=0)
                    values = jnp.concatenate([block[0, 1, h], block[1, 1, h]], axis=0)
                else:
                    keys, values = block[0, h], block[1, h]
                step(h, query, keys, values, False)

        total = l_ref[...]
        seen = total > 0.0
        safe = jnp.where(seen, total, 1.0)
        low = (acc_ref[...] / safe).astype(jnp.bfloat16)
        log_ref[h] = jnp.where(seen, m_ref[...] + jnp.log2(safe), LOW)
        for z in range(2):
            first, second = low[2 * z * rows : (2 * z + 1) * rows], low[(2 * z + 1) * rows : (2 * z + 2) * rows]
            keep_ref[z, h] = jnp.where(c == 0, first, second)
            send_ref[z, h] = jnp.where(c == 0, second, first)
        return carry

    lax.fori_loop(0, heads, head, 0)
    planes = put_logs([log_ref[h] for h in range(heads)], all_rows)
    for z in range(2):
        first, second = planes[2 * z * rows : (2 * z + 1) * rows], planes[(2 * z + 1) * rows : (2 * z + 2) * rows]
        keep_ref[z, heads] = jnp.where(c == 0, first, second)
        send_ref[z, heads] = jnp.where(c == 0, second, first)


def attend(idx, qo, qx, own, b1, b2, b3, b4, ring):
    _, heads, rows, size = qo.shape
    scale2 = size ** (-0.5) * math.log2(math.e)
    out = jax.ShapeDtypeStruct((2, heads + 1, rows, size), jnp.bfloat16)
    keys = 8 * rows
    return pl.pallas_call(
        functools.partial(attend_kernel, rows, heads, ring, scale2),
        out_shape=(out, out),
        in_specs=[SMEM] + [VMEM] * 7,
        out_specs=(VMEM, VMEM),
        scratch_shapes=[
            pltpu.VMEM((4 * rows, 1), jnp.float32),
            pltpu.VMEM((4 * rows, 1), jnp.float32),
            pltpu.VMEM((4 * rows, size), jnp.float32),
            pltpu.VMEM((heads, 4 * rows, 1), jnp.float32),
        ],
        compiler_params=PARAMS,
        cost_estimate=pl.CostEstimate(
            flops=4 * 4 * rows * keys * size * heads, bytes_accessed=4 << 20, transcendentals=4 * rows * keys * heads
        ),
        name="attend",
    )(idx, qo, qx, own, b1, b2, b3, b4)


def merge(first, second, heads):
    values, logs = [], []
    for h in range(heads):
        log_a, log_b = get_log(first[heads], h), get_log(second[heads], h)
        top = jnp.maximum(log_a, log_b)
        a, b = jnp.exp2(log_a - top), jnp.exp2(log_b - top)
        total = a + b
        value = (first[h].astype(jnp.float32) * a + second[h].astype(jnp.float32) * b) / total
        values.append(value.astype(jnp.bfloat16))
        logs.append(top + jnp.log2(total))
    return values, logs


def merge_core_kernel(heads, a_ref, b_ref, keep_ref, send_ref):
    for z, out_ref in enumerate((keep_ref, send_ref)):
        values, logs = merge(a_ref[z], b_ref[z], heads)
        for h in range(heads):
            out_ref[h] = values[h]
        out_ref[heads] = put_logs(logs, a_ref.shape[2])


def merge_far_kernel(heads, a_ref, b_ref, out_ref):
    values, _ = merge(a_ref[...], b_ref[...], heads)
    for h in range(heads):
        out_ref[h] = values[h]


def project_kernel(att_ref, w_ref, out_ref):
    cores, cols, heads, rows, size = att_ref.shape
    total = None
    for col in range(cols):
        for h in range(heads):
            left = jnp.concatenate([att_ref[core, col, h] for core in range(cores)], axis=0)
            right = w_ref[:, col * heads + h].reshape(size, w_ref.shape[3])
            term = jnp.dot(left, right, preferred_element_type=jnp.float32)
            total = term if total is None else total + term
    low = total.astype(jnp.bfloat16)
    for core in range(cores):
        out_ref[core] = low[core * rows : (core + 1) * rows]


def on_device(query_rows, key_rows, value_rows, out_weight, out_bias):
    rows, heads, size = query_rows.shape
    ring = lax.axis_size("y")
    y, zh, c = lax.axis_index("y"), lax.axis_index("zh"), lax.axis_index("c")
    idx = jnp.stack([y, zh, c]).astype(jnp.int32)
    swap = [(0, 1), (1, 0)]
    both = []
    for at in range(ring):
        both.append((2 * at, 2 * ((at + 1) % ring)))
        both.append((2 * at + 1, 2 * ((at - 1) % ring) + 1))

    def onward(block):
        return lax.ppermute(block, ("y", "c"), both)

    own = jnp.stack([jnp.swapaxes(key_rows, 0, 1), jnp.swapaxes(value_rows, 0, 1)])
    chip = lax.all_gather(own, "c", axis=0)
    b1 = onward(chip)
    qo = lax.all_gather(jnp.swapaxes(query_rows, 0, 1), "c", axis=0)
    qx = lax.ppermute(qo, "zh", swap)
    b2 = onward(b1)

    w_heads, w_deep, w_wide = out_weight.shape
    half = w_wide // 2
    w_core = lax.all_to_all(out_weight.reshape(w_heads, w_deep, 2, half), "c", 2, 0)
    w_far = lax.ppermute(w_core, "zh", swap)
    w_both = jnp.where(zh == 0, jnp.stack([w_core, w_far]), jnp.stack([w_far, w_core]))
    w_both = jnp.transpose(w_both, (2, 0, 1, 3, 4)).reshape(w_heads, 4 * w_deep, half)
    w_all = lax.all_gather(w_both, "y", axis=0)

    b3 = onward(b2)
    b4 = onward(lax.dynamic_index_in_dim(b3, c, 0, keepdims=False))
    keep, send = attend(idx, qo, qx, own, b1, b2, b3, b4, ring)
    other = lax.ppermute(send, "c", swap)
    part = jax.ShapeDtypeStruct((heads + 1, rows, size), jnp.bfloat16)
    keep, send = pl.pallas_call(
        functools.partial(merge_core_kernel, heads),
        out_shape=(part, part),
        in_specs=[VMEM, VMEM],
        out_specs=(VMEM, VMEM),
        compiler_params=PARAMS,
        name="merge_core",
    )(keep, other)
    other = lax.ppermute(send, "zh", swap)
    attended = pl.pallas_call(
        functools.partial(merge_far_kernel, heads),
        out_shape=jax.ShapeDtypeStruct((heads, rows, size), jnp.bfloat16),
        in_specs=[VMEM, VMEM],
        out_specs=VMEM,
        compiler_params=PARAMS,
        name="merge_far",
    )(keep, other)
    attended = lax.all_gather(attended, "col", axis=0)
    attended = lax.all_gather(attended, "c", axis=0)
    projected = pl.pallas_call(
        project_kernel,
        out_shape=jax.ShapeDtypeStruct((2, rows, half), jnp.bfloat16),
        in_specs=[VMEM, VMEM],
        out_specs=VMEM,
        compiler_params=PARAMS,
        name="project",
    )(attended, w_all)
    parts = lax.axis_size("row")
    pieces = projected.reshape(2 * parts, rows // parts, half)
    pieces = lax.all_to_all(pieces, ("c", "row"), 0, 0, tiled=True)
    pieces = pieces.reshape(2, parts, rows // parts, half)
    summed = jnp.sum(pieces.astype(jnp.float32), axis=1)
    summed = jnp.swapaxes(summed, 0, 1).reshape(rows // parts, w_wide)
    return (summed + out_bias[None, :]).astype(jnp.bfloat16)


def solution(mesh):
    shape = mesh.devices.shape
    fine = Mesh(mesh.devices.reshape((shape[0] // 4, 2, 2) + shape[1:]), ("y", "zh", "c", "row", "col"))
    seq = ("y", "zh", "c")
    in_specs = (
        P(seq, ("row", "col"), None),
        P(seq, ("row", "col"), None),
        P(seq, ("row", "col"), None),
        P("row", seq, "col"),
        P("col"),
    )
    out_specs = P(seq + ("row",), "col")
    return jax.shard_map(
        on_device, mesh=fine, in_specs=in_specs, out_specs=out_specs, check_vma=False
    )
```

```python
import functools
import math

import jax
import jax.numpy as jnp
from jax import lax
from jax.experimental import pallas as pl
from jax.experimental.pallas import tpu as pltpu
from jax.sharding import Mesh
from jax.sharding import PartitionSpec as P

LOW = -1e30
VMEM = pl.BlockSpec(memory_space=pltpu.VMEM)
SMEM = pl.BlockSpec(memory_space=pltpu.SMEM)
PARAMS = pltpu.CompilerParams(vmem_limit_bytes=48 * 1024 * 1024)


def split3(x):
    high = x.astype(jnp.bfloat16).astype(jnp.float32)
    rest = x - high
    mid = rest.astype(jnp.bfloat16).astype(jnp.float32)
    return high, mid, rest - mid


def first_state(m_ref, l_ref, acc_ref, h):
    m_ref[h] = jnp.full(m_ref.shape[1:], LOW, jnp.float32)
    l_ref[h] = jnp.zeros(l_ref.shape[1:], jnp.float32)
    acc_ref[h] = jnp.zeros(acc_ref.shape[1:], jnp.float32)


def attend_block(m_ref, l_ref, acc_ref, h, scale2, query, keys, values, allowed=None):
    scores = lax.dot_general(keys, query, (((1,), (1,)), ((), ())), preferred_element_type=jnp.float32)
    scores = scores * scale2
    if allowed is not None:
        scores = jnp.where(allowed, scores, LOW)
    old = m_ref[h]
    new = jnp.maximum(old, jnp.max(scores, axis=0, keepdims=True))
    weights = jnp.exp2(scores - new)
    if allowed is not None:
        weights = jnp.where(allowed, weights, 0.0)
    fade = jnp.exp2(old - new)
    m_ref[h] = new
    l_ref[h] = l_ref[h] * fade + jnp.sum(weights, axis=0, keepdims=True)
    acc_ref[h] = acc_ref[h] * fade + lax.dot_general(
        values, weights.astype(jnp.bfloat16), (((0,), (0,)), ((), ())), preferred_element_type=jnp.float32
    )


def chip_block(ref, h):
    keys = jnp.concatenate([ref[0, 0, h], ref[1, 0, h]], axis=0)
    values = jnp.concatenate([ref[0, 1, h], ref[1, 1, h]], axis=0)
    return keys, values


def source_of(idx_ref, ring, distance):
    y, c = idx_ref[0], idx_ref[2]
    return jnp.where(c == 0, y + ring - distance, y + distance) % ring


def pack_kernel(q_ref, k_ref, v_ref, w_ref, own_ref, qw_ref):
    heads, rows, size = q_ref.shape
    own_ref[0] = k_ref[...]
    own_ref[1] = v_ref[...]
    for h in range(heads):
        qw_ref[h * rows : (h + 1) * rows] = q_ref[h]
    w_heads, deep, wide = w_ref.shape
    group, tiles = 16 // deep, wide // 128
    for g in range(w_heads // group):
        lines = jnp.concatenate([w_ref[g * group + k].astype(jnp.float32) for k in range(group)], axis=0)
        lines = lines.astype(jnp.bfloat16)
        for t in range(tiles):
            at = heads * rows + (g * tiles + t) * 16
            qw_ref[at : at + 16] = lines[:, t * 128 : (t + 1) * 128]


def whole(shape):
    return pl.BlockSpec(shape, lambda i: (0,) * len(shape))


def pack(q, k, v, w):
    heads, rows, size = q.shape
    lines = heads * rows + math.prod(w.shape) // 128
    return pl.pallas_call(
        pack_kernel,
        out_shape=(
            jax.ShapeDtypeStruct((2, heads, rows, size), jnp.bfloat16),
            jax.ShapeDtypeStruct((lines, 128), jnp.bfloat16),
        ),
        grid=(1,),
        in_specs=[whole(x.shape) for x in (q, k, v, w)],
        out_specs=(whole((2, heads, rows, size)), whole((lines, 128))),
        compiler_params=pltpu.CompilerParams(vmem_limit_bytes=60 * 1024 * 1024),
        name="pack",
    )(q, k, v, w)


def unpack_kernel(heads, rows, deep, idx_ref, own_ref, far_ref, query_ref, w_ref):
    zh, c = idx_ref[1], idx_ref[2]
    first = zh == 0
    w_heads, _, half = w_ref.shape

    def lines(at, count):
        near = [own_ref[core, pl.ds(at, count), :] for core in range(2)]
        far = [far_ref[core, pl.ds(at, count), :] for core in range(2)]
        low = [jnp.where(first, a, b) for a, b in zip(near, far)]
        return low + [jnp.where(first, b, a) for a, b in zip(near, far)]

    for h in range(heads):
        for block, value in enumerate(lines(h * rows, rows)):
            query_ref[h, block * rows : (block + 1) * rows] = value
    group, tiles = 16 // deep, half // 128
    for g in range(w_heads // group):
        for t in range(tiles):
            tile = (g * 2 + c) * tiles + t
            wide = [x.astype(jnp.float32) for x in lines(pl.multiple_of(heads * rows + tile * 16, 16), 16)]
            for k in range(group):
                piece = jnp.concatenate([x[k * deep : (k + 1) * deep] for x in wide], axis=0).astype(jnp.bfloat16)
                w_ref[g * group + k, :, t * 128 : (t + 1) * 128] = piece


def unpack(idx, own, far, heads, rows, w_shape):
    w_heads, deep, wide = w_shape
    return pl.pallas_call(
        functools.partial(unpack_kernel, heads, rows, deep),
        out_shape=(
            jax.ShapeDtypeStruct((heads, 4 * rows, 128), jnp.bfloat16),
            jax.ShapeDtypeStruct((w_heads, 4 * deep, wide // 2), jnp.bfloat16),
        ),
        in_specs=[SMEM, VMEM, VMEM],
        out_specs=(VMEM, VMEM),
        compiler_params=PARAMS,
        name="unpack",
    )(idx, own, far)


def near_kernel(rows, heads, ring, scale2, idx_ref, q_ref, own_ref, b1_ref, b2_ref, m_ref, l_ref, acc_ref):
    y, zh, c = idx_ref[0], idx_ref[1], idx_ref[2]
    query_pos = lax.broadcasted_iota(jnp.int32, (1, 4 * rows), 1)
    key_pos = (zh * 2 + c) * rows + lax.broadcasted_iota(jnp.int32, (rows, 1), 0)
    allowed = key_pos <= query_pos
    for h in range(heads):
        first_state(m_ref, l_ref, acc_ref, h)
    for h in range(heads):
        attend_block(m_ref, l_ref, acc_ref, h, scale2, q_ref[h], own_ref[0, h], own_ref[1, h], allowed)
    for distance, block_ref in ((1, b1_ref), (2, b2_ref)):

        @pl.when(source_of(idx_ref, ring, distance) < y)
        def _():
            for h in range(heads):
                attend_block(m_ref, l_ref, acc_ref, h, scale2, q_ref[h], *chip_block(block_ref, h))


def far_kernel(
    rows, heads, ring, scale2, idx_ref, q_ref, b3_ref, b4_ref, m_in, l_in, acc_in,
    keep_ref, send_ref, m_ref, l_ref, acc_ref,
):
    y, zh, c = idx_ref[0], idx_ref[1], idx_ref[2]

    def put(z, at, first, second):
        place = jnp.where(zh == z, 0, 1)
        keep_ref[place, at : at + first.shape[0]] = jnp.where(c == 0, first, second)
        send_ref[place, at : at + first.shape[0]] = jnp.where(c == 0, second, first)

    m_ref[...] = m_in[...]
    l_ref[...] = l_in[...]
    acc_ref[...] = acc_in[...]

    @pl.when(source_of(idx_ref, ring, 3) < y)
    def _():
        for h in range(heads):
            attend_block(m_ref, l_ref, acc_ref, h, scale2, q_ref[h], *chip_block(b3_ref, h))

    @pl.when(source_of(idx_ref, ring, 4) < y)
    def _():
        for h in range(heads):
            attend_block(m_ref, l_ref, acc_ref, h, scale2, q_ref[h], b4_ref[0, h], b4_ref[1, h])

    line = lax.broadcasted_iota(jnp.int32, (16, 4 * rows), 0)
    plane = jnp.zeros((16, 4 * rows), jnp.float32)
    for h in range(heads):
        total = l_ref[h]
        seen = total > 0.0
        safe = jnp.where(seen, total, 1.0)
        low = jnp.transpose(acc_ref[h] * (1.0 / safe)).astype(jnp.bfloat16)
        for z in range(2):
            put(z, h * rows, low[2 * z * rows : (2 * z + 1) * rows], low[(2 * z + 1) * rows : (2 * z + 2) * rows])
        log = jnp.where(seen, m_ref[h] + jnp.log2(safe), LOW)
        for part, piece in enumerate(split3(log)):
            plane = jnp.where(line == 3 * h + part, piece, plane)
    plane = jnp.concatenate([plane, jnp.zeros((16, 128), jnp.float32)], axis=1)
    for z in range(2):
        first, second = [
            plane[:, block * rows : block * rows + 256].astype(jnp.bfloat16) for block in (2 * z, 2 * z + 1)
        ]
        put(z, heads * rows, first[:, :128], second[:, :128])
        put(z, heads * rows + 16, first[:, 128:], second[:, 128:])


def state_shapes(heads, rows, size, kind):
    return (
        kind((heads, 1, 4 * rows), jnp.float32),
        kind((heads, 1, 4 * rows), jnp.float32),
        kind((heads, size, 4 * rows), jnp.float32),
    )


def attend_near(idx, query, own, b1, b2, ring):
    heads, rows, size = query.shape[0], query.shape[1] // 4, query.shape[2]
    scale2 = size ** (-0.5) * math.log2(math.e)
    keys = 5 * rows
    return pl.pallas_call(
        functools.partial(near_kernel, rows, heads, ring, scale2),
        out_shape=state_shapes(heads, rows, size, jax.ShapeDtypeStruct),
        in_specs=[SMEM] + [VMEM] * 4,
        out_specs=(VMEM,) * 3,
        compiler_params=PARAMS,
        cost_estimate=pl.CostEstimate(
            flops=16 * rows * keys * size * heads, bytes_accessed=4 << 20, transcendentals=4 * rows * keys * heads
        ),
        name="attend_near",
    )(idx, query, own, b1, b2)


def attend_far(idx, query, b3, b4, state, ring):
    heads, rows, size = query.shape[0], query.shape[1] // 4, query.shape[2]
    scale2 = size ** (-0.5) * math.log2(math.e)
    out = jax.ShapeDtypeStruct((2, heads * rows + 32, size), jnp.bfloat16)
    keys = 3 * rows
    return pl.pallas_call(
        functools.partial(far_kernel, rows, heads, ring, scale2),
        out_shape=(out, out),
        in_specs=[SMEM] + [VMEM] * 6,
        out_specs=(VMEM, VMEM),
        scratch_shapes=state_shapes(heads, rows, size, pltpu.VMEM),
        compiler_params=PARAMS,
        cost_estimate=pl.CostEstimate(
            flops=16 * rows * keys * size * heads, bytes_accessed=4 << 20, transcendentals=4 * rows * keys * heads
        ),
        name="attend_far",
    )(idx, query, b3, b4, *state)


def merge_two(rows, heads, a, b, out_ref, last):
    at = heads * rows
    planes = [jnp.concatenate([x[at : at + 16], x[at + 16 : at + 32]], axis=1).astype(jnp.float32) for x in (a, b)]
    line = lax.broadcasted_iota(jnp.int32, (128, 256), 0)
    shares = jnp.zeros((128, 256), jnp.float32)
    logs = jnp.zeros((16, 256), jnp.float32)
    for h in range(heads):
        log_a, log_b = [p[3 * h : 3 * h + 1] + p[3 * h + 1 : 3 * h + 2] + p[3 * h + 2 : 3 * h + 3] for p in planes]
        top = jnp.maximum(log_a, log_b)
        part_a, part_b = jnp.exp2(log_a - top), jnp.exp2(log_b - top)
        total = part_a + part_b
        shares = jnp.where(line == 2 * h, part_a / total, shares)
        shares = jnp.where(line == 2 * h + 1, part_b / total, shares)
        for part, piece in enumerate(split3(top + jnp.log2(total))):
            logs = jnp.where(line[:16] == 3 * h + part, piece, logs)
    shares = jnp.transpose(shares)[:rows]
    for h in range(heads):
        value = a[h * rows : (h + 1) * rows].astype(jnp.float32) * shares[:, 2 * h : 2 * h + 1]
        value = value + b[h * rows : (h + 1) * rows].astype(jnp.float32) * shares[:, 2 * h + 1 : 2 * h + 2]
        out_ref[h * rows : (h + 1) * rows] = value.astype(jnp.bfloat16)
    if not last:
        low = logs.astype(jnp.bfloat16)
        out_ref[at : at + 16] = low[:, :128]
        out_ref[at + 16 : at + 32] = low[:, 128:]


def merge_core_kernel(rows, heads, a_ref, b_ref, keep_ref, send_ref):
    merge_two(rows, heads, a_ref[1], b_ref[1], send_ref, False)
    merge_two(rows, heads, a_ref[0], b_ref[0], keep_ref, False)


def merge_far_kernel(rows, heads, a_ref, b_ref, out_ref):
    merge_two(rows, heads, a_ref[...], b_ref[...], out_ref, True)


def merge_core(keep, other, heads):
    _, lines, size = keep.shape
    out = jax.ShapeDtypeStruct((lines, size), jnp.bfloat16)
    return pl.pallas_call(
        functools.partial(merge_core_kernel, (lines - 32) // heads, heads),
        out_shape=(out, out),
        in_specs=[VMEM, VMEM],
        out_specs=(VMEM, VMEM),
        compiler_params=PARAMS,
        name="merge_core",
    )(keep, other)


def merge_far(keep, other, heads):
    lines, size = keep.shape
    return pl.pallas_call(
        functools.partial(merge_far_kernel, (lines - 32) // heads, heads),
        out_shape=jax.ShapeDtypeStruct((lines - 32, size), jnp.bfloat16),
        in_specs=[VMEM, VMEM],
        out_specs=VMEM,
        compiler_params=PARAMS,
        name="merge_far",
    )(keep, other)


def project_kernel(hops, ring, idx_ref, att_ref, *refs):
    w_refs, out_ref, w_all = refs[: len(hops)], refs[-2], refs[-1]
    cores, heads, rows, size = att_ref.shape
    for hop, w_ref in zip(hops, w_refs):
        source = (idx_ref[0] + ring - hop) % ring
        for h in range(heads):
            w_all[h, source] = w_ref[h]
    total = None
    for h in range(heads):
        left = jnp.concatenate([att_ref[core, h] for core in range(cores)], axis=0)
        right = w_all[h].reshape(size, w_all.shape[3])
        term = jnp.dot(left, right, preferred_element_type=jnp.float32)
        total = term if total is None else total + term
    low = total.astype(jnp.bfloat16)
    for core in range(cores):
        out_ref[core] = low[core * rows : (core + 1) * rows]


def project(idx, attended, weights, ring):
    cores, heads, rows, _ = attended.shape
    _, deep, half = weights[0].shape
    return pl.pallas_call(
        functools.partial(project_kernel, tuple(weights), ring),
        out_shape=jax.ShapeDtypeStruct((cores, rows, half), jnp.bfloat16),
        in_specs=[SMEM] + [VMEM] * (1 + len(weights)),
        out_specs=VMEM,
        scratch_shapes=[pltpu.VMEM((heads, ring, deep, half), jnp.bfloat16)],
        compiler_params=PARAMS,
        name="project",
    )(idx, attended, *weights.values())


def on_device(query_rows, key_rows, value_rows, out_weight, out_bias):
    rows, heads, size = query_rows.shape
    ring = lax.axis_size("y")
    y, zh, c = lax.axis_index("y"), lax.axis_index("zh"), lax.axis_index("c")
    idx = jnp.stack([y, zh, c]).astype(jnp.int32)

    def onward(block, hops):
        pairs = []
        for at in range(ring):
            pairs.append((2 * at, 2 * ((at + hops) % ring)))
            pairs.append((2 * at + 1, 2 * ((at - hops) % ring) + 1))
        return lax.ppermute(block, ("y", "c"), pairs)

    own, qw = pack(
        jnp.swapaxes(query_rows, 0, 1), jnp.swapaxes(key_rows, 0, 1), jnp.swapaxes(value_rows, 0, 1), out_weight
    )
    chip = lax.all_gather(own, "c", axis=0)
    b1 = onward(chip, 1)
    b2 = onward(chip, 2)
    qw, _ = lax.optimization_barrier((qw, chip))
    qw_far = lax.ppermute(qw, "zh", [(0, 1), (1, 0)])
    qw_own = lax.all_gather(qw, "c", axis=0)
    qw_far = lax.all_gather(qw_far, "c", axis=0)
    b3 = onward(b2, 1)
    b4 = onward(lax.dynamic_index_in_dim(b2, c, 0, keepdims=False), 2)
    query, weight = unpack(idx, qw_own, qw_far, heads, rows, out_weight.shape)
    state = attend_near(idx, query, own, b1, b2, ring)

    def along(block, hops):
        return lax.ppermute(block, "y", [(at, (at + hops) % ring) for at in range(ring)])

    half = weight.shape[2]
    weight, state = lax.optimization_barrier((weight, state))
    weights = {0: weight}
    for hops in (1, -1, 2, -2):
        weights[hops] = along(weight, hops)
    weights[3] = along(weights[2], 1)
    weights[-3] = along(weights[-2], -1)
    weights[4] = along(weights[2], 2)
    keep, send = attend_far(idx, query, b3, b4, state, ring)
    keep, send = merge_core(keep, lax.ppermute(send, "c", [(0, 1), (1, 0)]), heads)
    attended = merge_far(keep, lax.ppermute(send, "zh", [(0, 1), (1, 0)]), heads)
    attended = attended.reshape(heads, rows, size)
    attended = lax.all_gather(attended, "col", axis=0, tiled=True)
    attended = lax.all_gather(attended, "c", axis=0)
    projected = project(idx, attended, weights, ring)
    parts = lax.axis_size("row")
    pieces = projected.reshape(2 * parts, rows // parts, half)
    pieces = lax.all_to_all(pieces, ("c", "row"), 0, 0, tiled=True)
    pieces = pieces.reshape(2, parts, rows // parts, half)
    summed = jnp.sum(pieces.astype(jnp.float32), axis=1)
    summed = jnp.swapaxes(summed, 0, 1).reshape(rows // parts, 2 * half)
    return (summed + out_bias[None, :]).astype(jnp.bfloat16)


def solution(mesh):
    shape = mesh.devices.shape
    fine = Mesh(mesh.devices.reshape((shape[0] // 4, 2, 2) + shape[1:]), ("y", "zh", "c", "row", "col"))
    seq = ("y", "zh", "c")
    in_specs = (
        P(seq, ("row", "col"), None),
        P(seq, ("row", "col"), None),
        P(seq, ("row", "col"), None),
        P("row", seq, "col"),
        P("col"),
    )
    out_specs = P(seq + ("row",), "col")
    return jax.shard_map(
        on_device, mesh=fine, in_specs=in_specs, out_specs=out_specs, check_vma=False
    )
```

```python
import functools
import math

import jax
import jax.numpy as jnp
from jax import lax
from jax.experimental import pallas as pl
from jax.experimental.pallas import tpu as pltpu
from jax.sharding import Mesh
from jax.sharding import PartitionSpec as P

LOW = -1e30
VMEM = pl.BlockSpec(memory_space=pltpu.VMEM)
SMEM = pl.BlockSpec(memory_space=pltpu.SMEM)
ROOMY = pltpu.CompilerParams(vmem_limit_bytes=60 * 1024 * 1024)
PARAMS = pltpu.CompilerParams(vmem_limit_bytes=48 * 1024 * 1024)


def split3(x):
    high = x.astype(jnp.bfloat16).astype(jnp.float32)
    rest = x - high
    mid = rest.astype(jnp.bfloat16).astype(jnp.float32)
    return high, mid, rest - mid


def first_state(m_ref, l_ref, acc_ref, h):
    m_ref[h] = jnp.full(m_ref.shape[1:], LOW, jnp.float32)
    l_ref[h] = jnp.zeros(l_ref.shape[1:], jnp.float32)
    acc_ref[h] = jnp.zeros(acc_ref.shape[1:], jnp.float32)


def attend_block(m_ref, l_ref, acc_ref, h, scale2, query, keys, values, allowed=None):
    scores = lax.dot_general(keys, query, (((1,), (1,)), ((), ())), preferred_element_type=jnp.float32)
    scores = scores * scale2
    if allowed is not None:
        scores = jnp.where(allowed, scores, LOW)
    old = m_ref[h]
    new = jnp.maximum(old, jnp.max(scores, axis=0, keepdims=True))
    weights = jnp.exp2(scores - new)
    if allowed is not None:
        weights = jnp.where(allowed, weights, 0.0)
    fade = jnp.exp2(old - new)
    m_ref[h] = new
    l_ref[h] = l_ref[h] * fade + jnp.sum(weights, axis=0, keepdims=True)
    acc_ref[h] = acc_ref[h] * fade + lax.dot_general(
        values, weights.astype(jnp.bfloat16), (((0,), (0,)), ((), ())), preferred_element_type=jnp.float32
    )


def chip_block(ref, h):
    keys = jnp.concatenate([ref[0, 0, h], ref[1, 0, h]], axis=0)
    values = jnp.concatenate([ref[0, 1, h], ref[1, 1, h]], axis=0)
    return keys, values


def source_of(idx_ref, ring, distance):
    y, c = idx_ref[0], idx_ref[2]
    return jnp.where(c == 0, y + ring - distance, y + distance) % ring


def whole(shape):
    return pl.BlockSpec(shape, lambda i: (0,) * len(shape))


def pack_kernel(q_ref, w_ref, qw_ref):
    heads, rows, size = q_ref.shape
    for h in range(heads):
        qw_ref[h * rows : (h + 1) * rows] = q_ref[h]
    w_heads, deep, wide = w_ref.shape
    group, tiles = 16 // deep, wide // 128
    for g in range(w_heads // group):
        lines = jnp.concatenate([w_ref[g * group + k].astype(jnp.float32) for k in range(group)], axis=0)
        lines = lines.astype(jnp.bfloat16)
        for t in range(tiles):
            at = heads * rows + (g * tiles + t) * 16
            qw_ref[at : at + 16] = lines[:, t * 128 : (t + 1) * 128]


def pack(q, w):
    heads, rows, size = q.shape
    lines = heads * rows + math.prod(w.shape) // 128
    return pl.pallas_call(
        pack_kernel,
        out_shape=jax.ShapeDtypeStruct((lines, 128), jnp.bfloat16),
        grid=(1,),
        in_specs=[whole(q.shape), whole(w.shape)],
        out_specs=whole((lines, 128)),
        compiler_params=ROOMY,
        name="pack",
    )(q, w)


def unpack_kernel(heads, rows, deep, idx_ref, own_ref, far_ref, query_ref, w_ref):
    first = idx_ref[1] == 0
    w_heads, _, wide = w_ref.shape

    def lines(at, count):
        near = [own_ref[core, at : at + count] for core in range(2)]
        far = [far_ref[core, at : at + count] for core in range(2)]
        low = [jnp.where(first, a, b) for a, b in zip(near, far)]
        return low + [jnp.where(first, b, a) for a, b in zip(near, far)]

    for h in range(heads):
        for block, value in enumerate(lines(h * rows, rows)):
            query_ref[h, block * rows : (block + 1) * rows] = value
    group, tiles = 16 // deep, wide // 128
    for g in range(w_heads // group):
        for t in range(tiles):
            tile = [x.astype(jnp.float32) for x in lines(heads * rows + (g * tiles + t) * 16, 16)]
            for k in range(group):
                piece = jnp.concatenate([x[k * deep : (k + 1) * deep] for x in tile], axis=0).astype(jnp.bfloat16)
                w_ref[g * group + k, :, t * 128 : (t + 1) * 128] = piece


def unpack(idx, own, far, heads, rows, w_shape):
    w_heads, deep, wide = w_shape
    return pl.pallas_call(
        functools.partial(unpack_kernel, heads, rows, deep),
        out_shape=(
            jax.ShapeDtypeStruct((heads, 4 * rows, 128), jnp.bfloat16),
            jax.ShapeDtypeStruct((w_heads, 4 * deep, wide), jnp.bfloat16),
        ),
        in_specs=[SMEM, VMEM, VMEM],
        out_specs=(VMEM, VMEM),
        compiler_params=PARAMS,
        name="unpack",
    )(idx, own, far)


def near_kernel(rows, heads, ring, scale2, idx_ref, q_ref, own_ref, b1_ref, b2_ref, m_ref, l_ref, acc_ref):
    y, zh, c = idx_ref[0], idx_ref[1], idx_ref[2]
    query_pos = lax.broadcasted_iota(jnp.int32, (1, 4 * rows), 1)
    key_pos = (zh * 2 + c) * rows + lax.broadcasted_iota(jnp.int32, (rows, 1), 0)
    allowed = key_pos <= query_pos
    for h in range(heads):
        first_state(m_ref, l_ref, acc_ref, h)
    for h in range(heads):
        attend_block(m_ref, l_ref, acc_ref, h, scale2, q_ref[h], own_ref[0, h], own_ref[1, h], allowed)
    for distance, block_ref in ((1, b1_ref), (2, b2_ref)):

        @pl.when(source_of(idx_ref, ring, distance) < y)
        def _():
            for h in range(heads):
                attend_block(m_ref, l_ref, acc_ref, h, scale2, q_ref[h], *chip_block(block_ref, h))


def far_kernel(
    rows, heads, ring, scale2, idx_ref, q_ref, b3_ref, b4_ref, m_in, l_in, acc_in,
    keep_ref, send_ref, m_ref, l_ref, acc_ref,
):
    y, zh, c = idx_ref[0], idx_ref[1], idx_ref[2]

    def put(z, at, first, second):
        place = jnp.where(zh == z, 0, 1)
        keep_ref[place, at : at + first.shape[0]] = jnp.where(c == 0, first, second)
        send_ref[place, at : at + first.shape[0]] = jnp.where(c == 0, second, first)

    m_ref[...] = m_in[...]
    l_ref[...] = l_in[...]
    acc_ref[...] = acc_in[...]

    @pl.when(source_of(idx_ref, ring, 3) < y)
    def _():
        for h in range(heads):
            attend_block(m_ref, l_ref, acc_ref, h, scale2, q_ref[h], *chip_block(b3_ref, h))

    @pl.when(source_of(idx_ref, ring, 4) < y)
    def _():
        for h in range(heads):
            attend_block(m_ref, l_ref, acc_ref, h, scale2, q_ref[h], b4_ref[0, h], b4_ref[1, h])

    line = lax.broadcasted_iota(jnp.int32, (16, 4 * rows), 0)
    plane = jnp.zeros((16, 4 * rows), jnp.float32)
    for h in range(heads):
        total = l_ref[h]
        seen = total > 0.0
        safe = jnp.where(seen, total, 1.0)
        low = jnp.transpose(acc_ref[h] * (1.0 / safe)).astype(jnp.bfloat16)
        for z in range(2):
            put(z, h * rows, low[2 * z * rows : (2 * z + 1) * rows], low[(2 * z + 1) * rows : (2 * z + 2) * rows])
        log = jnp.where(seen, m_ref[h] + jnp.log2(safe), LOW)
        for part, piece in enumerate(split3(log)):
            plane = jnp.where(line == 3 * h + part, piece, plane)
    plane = jnp.concatenate([plane, jnp.zeros((16, 128), jnp.float32)], axis=1)
    for z in range(2):
        first, second = [
            plane[:, block * rows : block * rows + 256].astype(jnp.bfloat16) for block in (2 * z, 2 * z + 1)
        ]
        put(z, heads * rows, first[:, :128], second[:, :128])
        put(z, heads * rows + 16, first[:, 128:], second[:, 128:])


def state_shapes(heads, rows, size, kind):
    return (
        kind((heads, 1, 4 * rows), jnp.float32),
        kind((heads, 1, 4 * rows), jnp.float32),
        kind((heads, size, 4 * rows), jnp.float32),
    )


def attend_near(idx, query, own, b1, b2, ring):
    heads, rows, size = query.shape[0], query.shape[1] // 4, query.shape[2]
    scale2 = size ** (-0.5) * math.log2(math.e)
    keys = 5 * rows
    return pl.pallas_call(
        functools.partial(near_kernel, rows, heads, ring, scale2),
        out_shape=state_shapes(heads, rows, size, jax.ShapeDtypeStruct),
        in_specs=[SMEM] + [VMEM] * 4,
        out_specs=(VMEM,) * 3,
        compiler_params=PARAMS,
        cost_estimate=pl.CostEstimate(
            flops=16 * rows * keys * size * heads, bytes_accessed=4 << 20, transcendentals=4 * rows * keys * heads
        ),
        name="attend_near",
    )(idx, query, own, b1, b2)


def attend_far(idx, query, b3, b4, state, ring):
    heads, rows, size = query.shape[0], query.shape[1] // 4, query.shape[2]
    scale2 = size ** (-0.5) * math.log2(math.e)
    out = jax.ShapeDtypeStruct((2, heads * rows + 32, size), jnp.bfloat16)
    keys = 3 * rows
    return pl.pallas_call(
        functools.partial(far_kernel, rows, heads, ring, scale2),
        out_shape=(out, out),
        in_specs=[SMEM] + [VMEM] * 6,
        out_specs=(VMEM, VMEM),
        scratch_shapes=state_shapes(heads, rows, size, pltpu.VMEM),
        compiler_params=PARAMS,
        cost_estimate=pl.CostEstimate(
            flops=16 * rows * keys * size * heads, bytes_accessed=4 << 20, transcendentals=4 * rows * keys * heads
        ),
        name="attend_far",
    )(idx, query, b3, b4, *state)


def merge_two(rows, heads, a, b, out_ref, last):
    at = heads * rows
    planes = [jnp.concatenate([x[at : at + 16], x[at + 16 : at + 32]], axis=1).astype(jnp.float32) for x in (a, b)]
    line = lax.broadcasted_iota(jnp.int32, (128, 256), 0)
    shares = jnp.zeros((128, 256), jnp.float32)
    logs = jnp.zeros((16, 256), jnp.float32)
    for h in range(heads):
        log_a, log_b = [p[3 * h : 3 * h + 1] + p[3 * h + 1 : 3 * h + 2] + p[3 * h + 2 : 3 * h + 3] for p in planes]
        top = jnp.maximum(log_a, log_b)
        part_a, part_b = jnp.exp2(log_a - top), jnp.exp2(log_b - top)
        total = part_a + part_b
        shares = jnp.where(line == 2 * h, part_a / total, shares)
        shares = jnp.where(line == 2 * h + 1, part_b / total, shares)
        for part, piece in enumerate(split3(top + jnp.log2(total))):
            logs = jnp.where(line[:16] == 3 * h + part, piece, logs)
    shares = jnp.transpose(shares)[:rows]
    for h in range(heads):
        value = a[h * rows : (h + 1) * rows].astype(jnp.float32) * shares[:, 2 * h : 2 * h + 1]
        value = value + b[h * rows : (h + 1) * rows].astype(jnp.float32) * shares[:, 2 * h + 1 : 2 * h + 2]
        out_ref[h * rows : (h + 1) * rows] = value.astype(jnp.bfloat16)
    if not last:
        low = logs.astype(jnp.bfloat16)
        out_ref[at : at + 16] = low[:, :128]
        out_ref[at + 16 : at + 32] = low[:, 128:]


def merge_core_kernel(rows, heads, a_ref, b_ref, keep_ref, send_ref):
    merge_two(rows, heads, a_ref[1], b_ref[1], send_ref, False)
    merge_two(rows, heads, a_ref[0], b_ref[0], keep_ref, False)


def merge_far_kernel(rows, heads, a_ref, b_ref, out_ref):
    merge_two(rows, heads, a_ref[...], b_ref[...], out_ref, True)


def merge_core(keep, other, heads):
    _, lines, size = keep.shape
    out = jax.ShapeDtypeStruct((lines, size), jnp.bfloat16)
    return pl.pallas_call(
        functools.partial(merge_core_kernel, (lines - 32) // heads, heads),
        out_shape=(out, out),
        in_specs=[VMEM, VMEM],
        out_specs=(VMEM, VMEM),
        compiler_params=PARAMS,
        name="merge_core",
    )(keep, other)


def merge_far(keep, other, heads):
    lines, size = keep.shape
    return pl.pallas_call(
        functools.partial(merge_far_kernel, (lines - 32) // heads, heads),
        out_shape=jax.ShapeDtypeStruct((lines - 32, size), jnp.bfloat16),
        in_specs=[VMEM, VMEM],
        out_specs=VMEM,
        compiler_params=PARAMS,
        name="merge_far",
    )(keep, other)


def project_kernel(ring, idx_ref, att_ref, w0_ref, w1_ref, w2_ref, w3_ref, w4_ref, keep_ref, send_ref):
    y, c = idx_ref[0], idx_ref[2]
    cores, heads, rows, size = att_ref.shape
    deep = w0_ref.shape[1]
    line = lax.broadcasted_iota(jnp.int32, (size, size), 0)
    lane = lax.broadcasted_iota(jnp.int32, (size, size), 1)
    sources = [jnp.where(c == 0, y, (y + 4) % ring)]
    for hops in (1, 2, 3):
        sources.append(jnp.where(c == 0, (y + ring - hops) % ring, (y + hops) % ring))
    moves = []
    for side in range(2):
        wanted = jnp.full((size, size), -1, jnp.int32)
        for slot, source in enumerate(sources):
            at = side * size // 2 + slot * deep
            inside = jnp.logical_and(lane >= at, lane < at + deep)
            wanted = jnp.where(inside, lane + (source * deep - at), wanted)
        moves.append(jnp.where(line == wanted, 1.0, 0.0).astype(jnp.bfloat16))
    total = None
    for h in range(0, heads, 2):
        left, right = None, []
        for side in range(2):
            columns = jnp.concatenate([att_ref[core, h + side] for core in range(cores)], axis=0)
            moved = jnp.dot(columns, moves[side], preferred_element_type=jnp.float32)
            left = moved if left is None else left + moved
            right.append(jnp.where(c == 0, w0_ref[h + side], w4_ref[h + side]))
            right += [ref[h + side] for ref in (w1_ref, w2_ref, w3_ref)]
        term = jnp.dot(left.astype(jnp.bfloat16), jnp.concatenate(right, axis=0), preferred_element_type=jnp.float32)
        total = term if total is None else total + term
    first, second = total[:rows], total[rows:]
    keep_ref[...] = jnp.where(c == 0, first, second)
    send_ref[...] = jnp.where(c == 0, second, first).astype(jnp.bfloat16)


def project(idx, attended, weights, ring):
    _, _, rows, _ = attended.shape
    shape = (rows, weights[0].shape[2])
    return pl.pallas_call(
        functools.partial(project_kernel, ring),
        out_shape=(jax.ShapeDtypeStruct(shape, jnp.float32), jax.ShapeDtypeStruct(shape, jnp.bfloat16)),
        in_specs=[SMEM] + [VMEM] * (1 + len(weights)),
        out_specs=(VMEM, VMEM),
        compiler_params=PARAMS,
        name="project",
    )(idx, attended, *weights)


def join_kernel(keep_ref, other_ref, out_ref):
    out_ref[...] = (keep_ref[...] + other_ref[...].astype(jnp.float32)).astype(jnp.bfloat16)


def join(keep, other):
    return pl.pallas_call(
        join_kernel,
        out_shape=jax.ShapeDtypeStruct(other.shape, jnp.bfloat16),
        in_specs=[VMEM, VMEM],
        out_specs=VMEM,
        compiler_params=PARAMS,
        name="join",
    )(keep, other)


def finish_kernel(pieces_ref, bias_ref, out_ref):
    total = pieces_ref[0].astype(jnp.float32)
    for part in range(1, pieces_ref.shape[0]):
        total = total + pieces_ref[part].astype(jnp.float32)
    out_ref[...] = (total + bias_ref[...]).astype(jnp.bfloat16)


def finish(pieces, bias):
    return pl.pallas_call(
        finish_kernel,
        out_shape=jax.ShapeDtypeStruct(pieces.shape[1:], jnp.bfloat16),
        in_specs=[VMEM, VMEM],
        out_specs=VMEM,
        compiler_params=PARAMS,
        name="finish",
    )(pieces, bias)


def on_device(query_rows, key_rows, value_rows, out_weight, out_bias):
    rows, heads, size = query_rows.shape
    ring = lax.axis_size("y")
    y, zh, c = lax.axis_index("y"), lax.axis_index("zh"), lax.axis_index("c")
    idx = jnp.stack([y, zh, c]).astype(jnp.int32)

    def onward(block, hops):
        pairs = []
        for at in range(ring):
            pairs.append((2 * at, 2 * ((at + hops) % ring)))
            pairs.append((2 * at + 1, 2 * ((at - hops) % ring) + 1))
        return lax.ppermute(block, ("y", "c"), pairs)

    swap = [(0, 1), (1, 0)]

    own = jnp.stack([jnp.swapaxes(key_rows, 0, 1), jnp.swapaxes(value_rows, 0, 1)])
    chip = lax.all_gather(own, "c", axis=0)
    b2 = onward(chip, 2)
    b1 = onward(chip, 1)
    query, weight, _ = lax.optimization_barrier((jnp.swapaxes(query_rows, 0, 1), out_weight, chip))
    qw = pack(query, weight)
    qw_far = lax.ppermute(qw, "zh", swap)
    qw_own = lax.all_gather(qw, "c", axis=0)
    qw_far = lax.all_gather(qw_far, "c", axis=0)
    b3 = onward(b2, 1)
    b4 = onward(lax.dynamic_index_in_dim(b2, c, 0, keepdims=False), 2)
    query, weight = unpack(idx, qw_own, qw_far, heads, rows, out_weight.shape)
    state = attend_near(idx, query, own, b1, b2, ring)

    weight, state, b3, b4 = lax.optimization_barrier((weight, state, b3, b4))
    w2 = onward(weight, 2)
    w1 = onward(weight, 1)
    keep, send = attend_far(idx, query, b3, b4, state, ring)
    keep, send = merge_core(keep, lax.ppermute(send, "c", swap), heads)
    other = lax.ppermute(send, "zh", swap)
    w2, other = lax.optimization_barrier((w2, other))
    w3 = onward(w2, 1)
    w4 = lax.ppermute(w2, ("y", "c"), [(2 * at + 1, 2 * ((at - 2) % ring) + 1) for at in range(ring)])
    attended = merge_far(keep, other, heads)
    attended = attended.reshape(heads, rows, size)
    attended = lax.all_gather(attended, "col", axis=0, tiled=True)
    attended = lax.all_gather(attended, "c", axis=0)
    keep, send = project(idx, attended, (weight, w1, w2, w3, w4), ring)
    joined = join(keep, lax.ppermute(send, "c", swap))
    parts = lax.axis_size("row")
    pieces = joined.reshape(parts, rows // parts, joined.shape[1])
    pieces = lax.all_to_all(pieces, "row", 0, 0, tiled=True)
    return finish(pieces, out_bias[None, :])


def solution(mesh):
    shape = mesh.devices.shape
    fine = Mesh(mesh.devices.reshape((shape[0] // 4, 2, 2) + shape[1:]), ("y", "zh", "c", "row", "col"))
    seq = ("y", "zh", "c")
    in_specs = (
        P(seq, ("row", "col"), None),
        P(seq, ("row", "col"), None),
        P(seq, ("row", "col"), None),
        P("row", seq, "col"),
        P("col"),
    )
    out_specs = P(seq + ("row",), "col")
    return jax.shard_map(
        on_device, mesh=fine, in_specs=in_specs, out_specs=out_specs, check_vma=False
    )
```

```python
import functools
import math

import jax
import jax.numpy as jnp
from jax import lax
from jax.experimental import pallas as pl
from jax.experimental.pallas import tpu as pltpu
from jax.sharding import Mesh
from jax.sharding import PartitionSpec as P

LOW = -1e30
VMEM = pl.BlockSpec(memory_space=pltpu.VMEM)
SMEM = pl.BlockSpec(memory_space=pltpu.SMEM)
ROOMY = pltpu.CompilerParams(vmem_limit_bytes=60 * 1024 * 1024)
PARAMS = pltpu.CompilerParams(vmem_limit_bytes=48 * 1024 * 1024)


def split3(x):
    high = x.astype(jnp.bfloat16).astype(jnp.float32)
    rest = x - high
    mid = rest.astype(jnp.bfloat16).astype(jnp.float32)
    return high, mid, rest - mid


def first_state(m_ref, l_ref, acc_ref, h):
    m_ref[h] = jnp.full(m_ref.shape[1:], LOW, jnp.float32)
    l_ref[h] = jnp.zeros(l_ref.shape[1:], jnp.float32)
    acc_ref[h] = jnp.zeros(acc_ref.shape[1:], jnp.float32)


def attend_block(m_ref, l_ref, acc_ref, h, scale2, query, keys, values, allowed=None):
    scores = lax.dot_general(keys, query, (((1,), (1,)), ((), ())), preferred_element_type=jnp.float32)
    scores = scores * scale2
    if allowed is not None:
        scores = jnp.where(allowed, scores, LOW)
    old = m_ref[h]
    new = jnp.maximum(old, jnp.max(scores, axis=0, keepdims=True))
    weights = jnp.exp2(scores - new)
    if allowed is not None:
        weights = jnp.where(allowed, weights, 0.0)
    fade = jnp.exp2(old - new)
    m_ref[h] = new
    l_ref[h] = l_ref[h] * fade + jnp.sum(weights, axis=0, keepdims=True)
    acc_ref[h] = acc_ref[h] * fade + lax.dot_general(
        values, weights.astype(jnp.bfloat16), (((0,), (0,)), ((), ())), preferred_element_type=jnp.float32
    )


def chip_block(ref, h):
    keys = jnp.concatenate([ref[0, 0, h], ref[1, 0, h]], axis=0)
    values = jnp.concatenate([ref[0, 1, h], ref[1, 1, h]], axis=0)
    return keys, values


def source_of(idx_ref, ring, distance):
    y, c = idx_ref[0], idx_ref[2]
    return jnp.where(c == 0, y + ring - distance, y + distance) % ring


def whole(shape):
    return pl.BlockSpec(shape, lambda i: (0,) * len(shape))


def pack_kernel(q_ref, w_ref, qw_ref):
    heads, rows, size = q_ref.shape
    for h in range(heads):
        qw_ref[h * rows : (h + 1) * rows] = q_ref[h]
    w_heads, deep, wide = w_ref.shape
    group, tiles = 16 // deep, wide // 128
    for g in range(w_heads // group):
        lines = jnp.concatenate([w_ref[g * group + k].astype(jnp.float32) for k in range(group)], axis=0)
        lines = lines.astype(jnp.bfloat16)
        for t in range(tiles):
            at = heads * rows + (g * tiles + t) * 16
            qw_ref[at : at + 16] = lines[:, t * 128 : (t + 1) * 128]


def pack(q, w):
    heads, rows, size = q.shape
    lines = heads * rows + math.prod(w.shape) // 128
    return pl.pallas_call(
        pack_kernel,
        out_shape=jax.ShapeDtypeStruct((lines, 128), jnp.bfloat16),
        grid=(1,),
        in_specs=[whole(q.shape), whole(w.shape)],
        out_specs=whole((lines, 128)),
        compiler_params=ROOMY,
        name="pack",
    )(q, w)


def unpack_kernel(heads, rows, deep, idx_ref, own_ref, far_ref, query_ref, w_ref):
    first = idx_ref[1] == 0
    w_heads, _, wide = w_ref.shape

    def lines(at, count):
        near = [own_ref[core, at : at + count] for core in range(2)]
        far = [far_ref[core, at : at + count] for core in range(2)]
        low = [jnp.where(first, a, b) for a, b in zip(near, far)]
        return low + [jnp.where(first, b, a) for a, b in zip(near, far)]

    for h in range(heads):
        for block, value in enumerate(lines(h * rows, rows)):
            query_ref[h, block * rows : (block + 1) * rows] = value
    group, tiles = 16 // deep, wide // 128
    for g in range(w_heads // group):
        for t in range(tiles):
            tile = [x.astype(jnp.float32) for x in lines(heads * rows + (g * tiles + t) * 16, 16)]
            for k in range(group):
                piece = jnp.concatenate([x[k * deep : (k + 1) * deep] for x in tile], axis=0).astype(jnp.bfloat16)
                w_ref[g * group + k, :, t * 128 : (t + 1) * 128] = piece


def unpack(idx, own, far, heads, rows, w_shape):
    w_heads, deep, wide = w_shape
    return pl.pallas_call(
        functools.partial(unpack_kernel, heads, rows, deep),
        out_shape=(
            jax.ShapeDtypeStruct((heads, 4 * rows, 128), jnp.bfloat16),
            jax.ShapeDtypeStruct((w_heads, 4 * deep, wide), jnp.bfloat16),
        ),
        in_specs=[SMEM, VMEM, VMEM],
        out_specs=(VMEM, VMEM),
        compiler_params=PARAMS,
        cost_estimate=pl.CostEstimate(flops=1 << 28, bytes_accessed=1 << 20, transcendentals=0),
        name="unpack",
    )(idx, own, far)


def near_kernel(rows, heads, ring, scale2, idx_ref, q_ref, own_ref, b1_ref, b2_ref, m_ref, l_ref, acc_ref):
    y, zh, c = idx_ref[0], idx_ref[1], idx_ref[2]
    query_pos = lax.broadcasted_iota(jnp.int32, (1, 4 * rows), 1)
    key_pos = (zh * 2 + c) * rows + lax.broadcasted_iota(jnp.int32, (rows, 1), 0)
    allowed = key_pos <= query_pos
    for h in range(heads):
        first_state(m_ref, l_ref, acc_ref, h)
    for h in range(heads):
        attend_block(m_ref, l_ref, acc_ref, h, scale2, q_ref[h], own_ref[0, h], own_ref[1, h], allowed)
    for distance, block_ref in ((1, b1_ref), (2, b2_ref)):

        @pl.when(source_of(idx_ref, ring, distance) < y)
        def _():
            for h in range(heads):
                attend_block(m_ref, l_ref, acc_ref, h, scale2, q_ref[h], *chip_block(block_ref, h))


def far_kernel(
    rows, heads, ring, scale2, idx_ref, q_ref, b3_ref, b4_ref, m_in, l_in, acc_in,
    keep_ref, send_ref, m_ref, l_ref, acc_ref,
):
    y, zh, c = idx_ref[0], idx_ref[1], idx_ref[2]

    def put(z, at, first, second):
        place = jnp.where(zh == z, 0, 1)
        keep_ref[place, at : at + first.shape[0]] = jnp.where(c == 0, first, second)
        send_ref[place, at : at + first.shape[0]] = jnp.where(c == 0, second, first)

    m_ref[...] = m_in[...]
    l_ref[...] = l_in[...]
    acc_ref[...] = acc_in[...]

    @pl.when(source_of(idx_ref, ring, 3) < y)
    def _():
        for h in range(heads):
            attend_block(m_ref, l_ref, acc_ref, h, scale2, q_ref[h], *chip_block(b3_ref, h))

    @pl.when(source_of(idx_ref, ring, 4) < y)
    def _():
        for h in range(heads):
            attend_block(m_ref, l_ref, acc_ref, h, scale2, q_ref[h], b4_ref[0, h], b4_ref[1, h])

    line = lax.broadcasted_iota(jnp.int32, (16, 4 * rows), 0)
    plane = jnp.zeros((16, 4 * rows), jnp.float32)
    for h in range(heads):
        total = l_ref[h]
        seen = total > 0.0
        safe = jnp.where(seen, total, 1.0)
        low = jnp.transpose(acc_ref[h] * (1.0 / safe)).astype(jnp.bfloat16)
        for z in range(2):
            put(z, h * rows, low[2 * z * rows : (2 * z + 1) * rows], low[(2 * z + 1) * rows : (2 * z + 2) * rows])
        log = jnp.where(seen, m_ref[h] + jnp.log2(safe), LOW)
        for part, piece in enumerate(split3(log)):
            plane = jnp.where(line == 3 * h + part, piece, plane)
    plane = jnp.concatenate([plane, jnp.zeros((16, 128), jnp.float32)], axis=1)
    for z in range(2):
        first, second = [
            plane[:, block * rows : block * rows + 256].astype(jnp.bfloat16) for block in (2 * z, 2 * z + 1)
        ]
        put(z, heads * rows, first[:, :128], second[:, :128])
        put(z, heads * rows + 16, first[:, 128:], second[:, 128:])


def state_shapes(heads, rows, size, kind):
    return (
        kind((heads, 1, 4 * rows), jnp.float32),
        kind((heads, 1, 4 * rows), jnp.float32),
        kind((heads, size, 4 * rows), jnp.float32),
    )


def attend_near(idx, query, own, b1, b2, ring):
    heads, rows, size = query.shape[0], query.shape[1] // 4, query.shape[2]
    scale2 = size ** (-0.5) * math.log2(math.e)
    keys = 5 * rows
    return pl.pallas_call(
        functools.partial(near_kernel, rows, heads, ring, scale2),
        out_shape=state_shapes(heads, rows, size, jax.ShapeDtypeStruct),
        in_specs=[SMEM] + [VMEM] * 4,
        out_specs=(VMEM,) * 3,
        compiler_params=PARAMS,
        cost_estimate=pl.CostEstimate(flops=1 << 28, bytes_accessed=1 << 18, transcendentals=0),
        name="attend_near",
    )(idx, query, own, b1, b2)


def attend_far(idx, query, b3, b4, state, ring):
    heads, rows, size = query.shape[0], query.shape[1] // 4, query.shape[2]
    scale2 = size ** (-0.5) * math.log2(math.e)
    out = jax.ShapeDtypeStruct((2, heads * rows + 32, size), jnp.bfloat16)
    keys = 3 * rows
    return pl.pallas_call(
        functools.partial(far_kernel, rows, heads, ring, scale2),
        out_shape=(out, out),
        in_specs=[SMEM] + [VMEM] * 6,
        out_specs=(VMEM, VMEM),
        scratch_shapes=state_shapes(heads, rows, size, pltpu.VMEM),
        compiler_params=PARAMS,
        cost_estimate=pl.CostEstimate(
            flops=16 * rows * keys * size * heads, bytes_accessed=4 << 20, transcendentals=4 * rows * keys * heads
        ),
        name="attend_far",
    )(idx, query, b3, b4, *state)


def merge_two(rows, heads, a, b, out_ref, last):
    at = heads * rows
    planes = [jnp.concatenate([x[at : at + 16], x[at + 16 : at + 32]], axis=1).astype(jnp.float32) for x in (a, b)]
    line = lax.broadcasted_iota(jnp.int32, (128, 256), 0)
    shares = jnp.zeros((128, 256), jnp.float32)
    logs = jnp.zeros((16, 256), jnp.float32)
    for h in range(heads):
        log_a, log_b = [p[3 * h : 3 * h + 1] + p[3 * h + 1 : 3 * h + 2] + p[3 * h + 2 : 3 * h + 3] for p in planes]
        top = jnp.maximum(log_a, log_b)
        part_a, part_b = jnp.exp2(log_a - top), jnp.exp2(log_b - top)
        total = part_a + part_b
        shares = jnp.where(line == 2 * h, part_a / total, shares)
        shares = jnp.where(line == 2 * h + 1, part_b / total, shares)
        for part, piece in enumerate(split3(top + jnp.log2(total))):
            logs = jnp.where(line[:16] == 3 * h + part, piece, logs)
    shares = jnp.transpose(shares)[:rows]
    for h in range(heads):
        value = a[h * rows : (h + 1) * rows].astype(jnp.float32) * shares[:, 2 * h : 2 * h + 1]
        value = value + b[h * rows : (h + 1) * rows].astype(jnp.float32) * shares[:, 2 * h + 1 : 2 * h + 2]
        out_ref[h * rows : (h + 1) * rows] = value.astype(jnp.bfloat16)
    if not last:
        low = logs.astype(jnp.bfloat16)
        out_ref[at : at + 16] = low[:, :128]
        out_ref[at + 16 : at + 32] = low[:, 128:]


def merge_core_kernel(rows, heads, a_ref, b_ref, keep_ref, send_ref):
    merge_two(rows, heads, a_ref[1], b_ref[1], send_ref, False)
    merge_two(rows, heads, a_ref[0], b_ref[0], keep_ref, False)


def merge_far_kernel(rows, heads, a_ref, b_ref, out_ref):
    merge_two(rows, heads, a_ref[...], b_ref[...], out_ref, True)


def merge_core(keep, other, heads):
    _, lines, size = keep.shape
    out = jax.ShapeDtypeStruct((lines, size), jnp.bfloat16)
    return pl.pallas_call(
        functools.partial(merge_core_kernel, (lines - 32) // heads, heads),
        out_shape=(out, out),
        in_specs=[VMEM, VMEM],
        out_specs=(VMEM, VMEM),
        compiler_params=PARAMS,
        name="merge_core",
    )(keep, other)


def merge_far(keep, other, heads):
    lines, size = keep.shape
    return pl.pallas_call(
        functools.partial(merge_far_kernel, (lines - 32) // heads, heads),
        out_shape=jax.ShapeDtypeStruct((lines - 32, size), jnp.bfloat16),
        in_specs=[VMEM, VMEM],
        out_specs=VMEM,
        compiler_params=PARAMS,
        cost_estimate=pl.CostEstimate(flops=1 << 31, bytes_accessed=7 << 20, transcendentals=0),
        name="merge_far",
    )(keep, other)


def project_kernel(ring, idx_ref, att_ref, w0_ref, w1_ref, w2_ref, w3_ref, w4_ref, keep_ref, send_ref):
    y, c = idx_ref[0], idx_ref[2]
    cores, heads, rows, size = att_ref.shape
    deep = w0_ref.shape[1]
    line = lax.broadcasted_iota(jnp.int32, (size, size), 0)
    lane = lax.broadcasted_iota(jnp.int32, (size, size), 1)
    sources = [jnp.where(c == 0, y, (y + 4) % ring)]
    for hops in (1, 2, 3):
        sources.append(jnp.where(c == 0, (y + ring - hops) % ring, (y + hops) % ring))
    moves = []
    for side in range(2):
        wanted = jnp.full((size, size), -1, jnp.int32)
        for slot, source in enumerate(sources):
            at = side * size // 2 + slot * deep
            inside = jnp.logical_and(lane >= at, lane < at + deep)
            wanted = jnp.where(inside, lane + (source * deep - at), wanted)
        moves.append(jnp.where(line == wanted, 1.0, 0.0).astype(jnp.bfloat16))
    lefts, rights = [], []
    for h in range(0, heads, 2):
        left = None
        for side in range(2):
            columns = jnp.concatenate([att_ref[core, h + side] for core in range(cores)], axis=0)
            moved = jnp.dot(columns, moves[side], preferred_element_type=jnp.float32)
            left = moved if left is None else left + moved
            rights.append((w0_ref, w4_ref, h + side))
            rights += [(ref, None, h + side) for ref in (w1_ref, w2_ref, w3_ref)]
        lefts.append(left.astype(jnp.bfloat16))
    left = jnp.concatenate(lefts, axis=1)
    wide = w0_ref.shape[2]
    for at in range(0, wide, 256):
        pieces = []
        for ref, other, h in rights:
            piece = ref[h, :, at : at + 256]
            pieces.append(piece if other is None else jnp.where(c == 0, piece, other[h, :, at : at + 256]))
        total = jnp.dot(left, jnp.concatenate(pieces, axis=0), preferred_element_type=jnp.float32)
        first, second = total[:rows], total[rows:]
        keep_ref[:, at : at + 256] = jnp.where(c == 0, first, second)
        send_ref[:, at : at + 256] = jnp.where(c == 0, second, first).astype(jnp.bfloat16)


def project(idx, attended, weights, ring):
    _, _, rows, _ = attended.shape
    shape = (rows, weights[0].shape[2])
    return pl.pallas_call(
        functools.partial(project_kernel, ring),
        out_shape=(jax.ShapeDtypeStruct(shape, jnp.float32), jax.ShapeDtypeStruct(shape, jnp.bfloat16)),
        in_specs=[SMEM] + [VMEM] * (1 + len(weights)),
        out_specs=(VMEM, VMEM),
        compiler_params=PARAMS,
        name="project",
    )(idx, attended, *weights)


def join_kernel(keep_ref, other_ref, out_ref):
    out_ref[...] = (keep_ref[...] + other_ref[...].astype(jnp.float32)).astype(jnp.bfloat16)


def join(keep, other):
    return pl.pallas_call(
        join_kernel,
        out_shape=jax.ShapeDtypeStruct(other.shape, jnp.bfloat16),
        in_specs=[VMEM, VMEM],
        out_specs=VMEM,
        compiler_params=PARAMS,
        name="join",
    )(keep, other)


def finish_kernel(pieces_ref, bias_ref, out_ref):
    total = pieces_ref[0].astype(jnp.float32)
    for part in range(1, pieces_ref.shape[0]):
        total = total + pieces_ref[part].astype(jnp.float32)
    out_ref[...] = (total + bias_ref[...]).astype(jnp.bfloat16)


def finish(pieces, bias):
    return pl.pallas_call(
        finish_kernel,
        out_shape=jax.ShapeDtypeStruct(pieces.shape[1:], jnp.bfloat16),
        in_specs=[VMEM, VMEM],
        out_specs=VMEM,
        compiler_params=PARAMS,
        name="finish",
    )(pieces, bias)


def on_device(query_rows, key_rows, value_rows, out_weight, out_bias):
    rows, heads, size = query_rows.shape
    ring = lax.axis_size("y")
    y, zh, c = lax.axis_index("y"), lax.axis_index("zh"), lax.axis_index("c")
    idx = jnp.stack([y, zh, c]).astype(jnp.int32)

    def onward(block, hops):
        pairs = []
        for at in range(ring):
            pairs.append((2 * at, 2 * ((at + hops) % ring)))
            pairs.append((2 * at + 1, 2 * ((at - hops) % ring) + 1))
        return lax.ppermute(block, ("y", "c"), pairs)

    swap = [(0, 1), (1, 0)]

    own = jnp.stack([jnp.swapaxes(key_rows, 0, 1), jnp.swapaxes(value_rows, 0, 1)])
    chip = lax.all_gather(own, "c", axis=0)
    b2 = onward(chip, 2)
    query, weight, _ = lax.optimization_barrier((jnp.swapaxes(query_rows, 0, 1), out_weight, chip))
    qw = pack(query, weight)
    near_chip, qw = lax.optimization_barrier((chip, qw))
    b1 = onward(near_chip, 1)
    qw_far = lax.ppermute(qw, "zh", swap)
    qw_own = lax.all_gather(qw, "c", axis=0)
    qw_far = lax.all_gather(qw_far, "c", axis=0)
    b2, qw_own = lax.optimization_barrier((b2, qw_own))
    b3 = onward(b2, 1)
    b4 = onward(lax.dynamic_index_in_dim(b2, c, 0, keepdims=False), 2)
    query, weight = unpack(idx, qw_own, qw_far, heads, rows, out_weight.shape)
    state = attend_near(idx, query, own, b1, b2, ring)

    weight, state = lax.optimization_barrier((weight, state))
    w2 = onward(weight, 2)
    w1 = onward(weight, 1)
    keep, send = attend_far(idx, query, b3, b4, state, ring)
    keep, send = merge_core(keep, lax.ppermute(send, "c", swap), heads)
    other = lax.ppermute(send, "zh", swap)
    w3 = onward(w2, 1)
    w4 = lax.ppermute(w2, ("y", "c"), [(2 * at + 1, 2 * ((at - 2) % ring) + 1) for at in range(ring)])
    attended = merge_far(keep, other, heads)
    attended = attended.reshape(heads, rows, size)
    attended = lax.all_gather(attended, "col", axis=0, tiled=True)
    attended = lax.all_gather(attended, "c", axis=0)
    keep, send = project(idx, attended, (weight, w1, w2, w3, w4), ring)
    joined = join(keep, lax.ppermute(send, "c", swap))
    parts = lax.axis_size("row")
    pieces = joined.reshape(parts, rows // parts, joined.shape[1])
    pieces = lax.all_to_all(pieces, "row", 0, 0, tiled=True)
    return finish(pieces, out_bias[None, :])


def solution(mesh):
    shape = mesh.devices.shape
    fine = Mesh(mesh.devices.reshape((shape[0] // 4, 2, 2) + shape[1:]), ("y", "zh", "c", "row", "col"))
    seq = ("y", "zh", "c")
    in_specs = (
        P(seq, ("row", "col"), None),
        P(seq, ("row", "col"), None),
        P(seq, ("row", "col"), None),
        P("row", seq, "col"),
        P("col"),
    )
    out_specs = P(seq + ("row",), "col")
    return jax.shard_map(
        on_device, mesh=fine, in_specs=in_specs, out_specs=out_specs, check_vma=False
    )
```

```python
import functools
import math

import jax
import jax.numpy as jnp
from jax import lax
from jax.experimental import pallas as pl
from jax.experimental.pallas import tpu as pltpu
from jax.sharding import Mesh
from jax.sharding import PartitionSpec as P

LOW = -1e30
VMEM = pl.BlockSpec(memory_space=pltpu.VMEM)
SMEM = pl.BlockSpec(memory_space=pltpu.SMEM)
ROOMY = pltpu.CompilerParams(vmem_limit_bytes=60 * 1024 * 1024)
PARAMS = pltpu.CompilerParams(vmem_limit_bytes=48 * 1024 * 1024)


def split3(x):
    high = x.astype(jnp.bfloat16).astype(jnp.float32)
    rest = x - high
    mid = rest.astype(jnp.bfloat16).astype(jnp.float32)
    return high, mid, rest - mid


def attend_block(state, scale2, query, keys, values, seen, allowed=None):
    scores = lax.dot_general(keys, query, (((1,), (1,)), ((), ())), preferred_element_type=jnp.float32)
    if allowed is not None:
        scores = jnp.where(allowed, scores, LOW)
    top = jnp.where(seen, jnp.max(scores, axis=0, keepdims=True) * scale2, LOW)
    new = top if state is None else jnp.maximum(state[0], top)
    shift = jnp.where(jnp.logical_and(new > 0.5 * LOW, seen), new, -LOW)
    weights = jnp.exp2(scores * scale2 - shift)
    total = jnp.sum(weights, axis=0, keepdims=True)
    sums = lax.dot_general(
        values, weights.astype(jnp.bfloat16), (((0,), (0,)), ((), ())), preferred_element_type=jnp.float32
    )
    if state is None:
        return new, total, sums
    fade = jnp.exp2(state[0] - new)
    return new, state[1] * fade + total, state[2] * fade + sums


def chip_block(ref, h):
    keys = jnp.concatenate([ref[0, 0, h], ref[1, 0, h]], axis=0)
    values = jnp.concatenate([ref[0, 1, h], ref[1, 1, h]], axis=0)
    return keys, values


def source_of(idx_ref, ring, distance):
    y, c = idx_ref[0], idx_ref[2]
    return jnp.where(c == 0, y + ring - distance, y + distance) % ring


def whole(shape):
    return pl.BlockSpec(shape, lambda i: (0,) * len(shape))


def pack_kernel(q_ref, w_ref, qw_ref):
    heads, rows, size = q_ref.shape
    for h in range(heads):
        qw_ref[h * rows : (h + 1) * rows] = q_ref[h]
    w_heads, deep, wide = w_ref.shape
    group, tiles = 16 // deep, wide // 128
    for g in range(w_heads // group):
        lines = jnp.concatenate([w_ref[g * group + k].astype(jnp.float32) for k in range(group)], axis=0)
        lines = lines.astype(jnp.bfloat16)
        for t in range(tiles):
            at = heads * rows + (g * tiles + t) * 16
            qw_ref[at : at + 16] = lines[:, t * 128 : (t + 1) * 128]


def pack(q, w):
    heads, rows, size = q.shape
    lines = heads * rows + math.prod(w.shape) // 128
    return pl.pallas_call(
        pack_kernel,
        out_shape=jax.ShapeDtypeStruct((lines, 128), jnp.bfloat16),
        grid=(1,),
        in_specs=[whole(q.shape), whole(w.shape)],
        out_specs=whole((lines, 128)),
        compiler_params=ROOMY,
        name="pack",
    )(q, w)


def unpack_kernel(heads, rows, deep, idx_ref, own_ref, far_ref, query_ref, w_ref):
    first = idx_ref[1] == 0
    w_heads, _, wide = w_ref.shape
    turn = jnp.where(idx_ref[2] == 0, w_heads // 2, 0)

    def lines(at, count):
        near = [own_ref[core, at : at + count] for core in range(2)]
        far = [far_ref[core, at : at + count] for core in range(2)]
        low = [jnp.where(first, a, b) for a, b in zip(near, far)]
        return low + [jnp.where(first, b, a) for a, b in zip(near, far)]

    for h in range(heads):
        for block, value in enumerate(lines(h * rows, rows)):
            query_ref[h, block * rows : (block + 1) * rows] = value
    group, tiles = 16 // deep, wide // 128
    for g in range(w_heads // group):
        for t in range(tiles):
            tile = [x.astype(jnp.float32) for x in lines(heads * rows + (g * tiles + t) * 16, 16)]
            for k in range(group):
                piece = jnp.concatenate([x[k * deep : (k + 1) * deep] for x in tile], axis=0).astype(jnp.bfloat16)
                w_ref[(g * group + k + turn) % w_heads, :, t * 128 : (t + 1) * 128] = piece


def unpack(idx, own, far, heads, rows, w_shape):
    w_heads, deep, wide = w_shape
    return pl.pallas_call(
        functools.partial(unpack_kernel, heads, rows, deep),
        out_shape=(
            jax.ShapeDtypeStruct((heads, 4 * rows, 128), jnp.bfloat16),
            jax.ShapeDtypeStruct((w_heads, 4 * deep, wide), jnp.bfloat16),
        ),
        in_specs=[SMEM, VMEM, VMEM],
        out_specs=(VMEM, VMEM),
        compiler_params=PARAMS,
        cost_estimate=pl.CostEstimate(flops=1 << 28, bytes_accessed=1 << 20, transcendentals=0),
        name="unpack",
    )(idx, own, far)


def near_kernel(rows, heads, ring, scale2, idx_ref, q_ref, own_ref, b1_ref, b2_ref, m_ref, l_ref, acc_ref):
    y, zh, c = idx_ref[0], idx_ref[1], idx_ref[2]
    query_pos = lax.broadcasted_iota(jnp.int32, (1, 4 * rows), 1)
    key_pos = (zh * 2 + c) * rows + lax.broadcasted_iota(jnp.int32, (rows, 1), 0)
    own_seen = query_pos >= (zh * 2 + c) * rows
    for h in range(heads):
        query = q_ref[h]
        state = attend_block(
            None, scale2, query, own_ref[0, h], own_ref[1, h], own_seen, key_pos <= query_pos
        )
        for distance, block_ref in ((1, b1_ref), (2, b2_ref)):
            seen = source_of(idx_ref, ring, distance) < y
            state = attend_block(state, scale2, query, *chip_block(block_ref, h), seen)
        m_ref[h], l_ref[h], acc_ref[h] = state


def far_kernel(rows, heads, ring, scale2, idx_ref, q_ref, b3_ref, b4_ref, m_ref, l_ref, acc_ref, keep_ref, send_ref):
    y, zh, c = idx_ref[0], idx_ref[1], idx_ref[2]

    def put(z, at, first, second):
        place = jnp.where(zh == z, 0, 1)
        keep_ref[place, at : at + first.shape[0]] = jnp.where(c == 0, first, second)
        send_ref[place, at : at + first.shape[0]] = jnp.where(c == 0, second, first)

    line = lax.broadcasted_iota(jnp.int32, (16, 4 * rows), 0)
    plane = jnp.zeros((16, 4 * rows), jnp.float32)
    for h in range(heads):
        query = q_ref[h]
        state = m_ref[h], l_ref[h], acc_ref[h]
        seen = source_of(idx_ref, ring, 4) < y
        state = attend_block(state, scale2, query, b4_ref[0, h], b4_ref[1, h], seen)
        seen = source_of(idx_ref, ring, 3) < y
        most, total, sums = attend_block(state, scale2, query, *chip_block(b3_ref, h), seen)
        seen = total > 0.0
        safe = jnp.where(seen, total, 1.0)
        low = jnp.transpose(sums * (1.0 / safe)).astype(jnp.bfloat16)
        for z in range(2):
            put(z, h * rows, low[2 * z * rows : (2 * z + 1) * rows], low[(2 * z + 1) * rows : (2 * z + 2) * rows])
        log = jnp.where(seen, most + jnp.log2(safe), LOW)
        for part, piece in enumerate(split3(log)):
            plane = jnp.where(line == 3 * h + part, piece, plane)
    plane = jnp.concatenate([plane, jnp.zeros((16, 128), jnp.float32)], axis=1)
    for z in range(2):
        first, second = [
            plane[:, block * rows : block * rows + 256].astype(jnp.bfloat16) for block in (2 * z, 2 * z + 1)
        ]
        put(z, heads * rows, first[:, :128], second[:, :128])
        put(z, heads * rows + 16, first[:, 128:], second[:, 128:])


def state_shapes(heads, rows, size, kind):
    return (
        kind((heads, 1, 4 * rows), jnp.float32),
        kind((heads, 1, 4 * rows), jnp.float32),
        kind((heads, size, 4 * rows), jnp.float32),
    )


def attend_near(idx, query, own, b1, b2, ring):
    heads, rows, size = query.shape[0], query.shape[1] // 4, query.shape[2]
    scale2 = size ** (-0.5) * math.log2(math.e)
    keys = 5 * rows
    return pl.pallas_call(
        functools.partial(near_kernel, rows, heads, ring, scale2),
        out_shape=state_shapes(heads, rows, size, jax.ShapeDtypeStruct),
        in_specs=[SMEM] + [VMEM] * 4,
        out_specs=(VMEM,) * 3,
        compiler_params=PARAMS,
        cost_estimate=pl.CostEstimate(flops=1 << 28, bytes_accessed=1 << 18, transcendentals=0),
        name="attend_near",
    )(idx, query, own, b1, b2)


def attend_far(idx, query, b3, b4, state, ring):
    heads, rows, size = query.shape[0], query.shape[1] // 4, query.shape[2]
    scale2 = size ** (-0.5) * math.log2(math.e)
    out = jax.ShapeDtypeStruct((2, heads * rows + 32, size), jnp.bfloat16)
    keys = 3 * rows
    return pl.pallas_call(
        functools.partial(far_kernel, rows, heads, ring, scale2),
        out_shape=(out, out),
        in_specs=[SMEM] + [VMEM] * 6,
        out_specs=(VMEM, VMEM),
        compiler_params=PARAMS,
        cost_estimate=pl.CostEstimate(
            flops=16 * rows * keys * size * heads, bytes_accessed=4 << 20, transcendentals=4 * rows * keys * heads
        ),
        name="attend_far",
    )(idx, query, b3, b4, *state)


def merge_two(rows, heads, a, b, out_ref, last):
    at = heads * rows
    planes = [jnp.concatenate([x[at : at + 16], x[at + 16 : at + 32]], axis=1).astype(jnp.float32) for x in (a, b)]
    line = lax.broadcasted_iota(jnp.int32, (128, 256), 0)
    shares = jnp.zeros((128, 256), jnp.float32)
    logs = jnp.zeros((16, 256), jnp.float32)
    for h in range(heads):
        log_a, log_b = [p[3 * h : 3 * h + 1] + p[3 * h + 1 : 3 * h + 2] + p[3 * h + 2 : 3 * h + 3] for p in planes]
        top = jnp.maximum(log_a, log_b)
        part_a, part_b = jnp.exp2(log_a - top), jnp.exp2(log_b - top)
        total = part_a + part_b
        shares = jnp.where(line == 2 * h, part_a / total, shares)
        shares = jnp.where(line == 2 * h + 1, part_b / total, shares)
        for part, piece in enumerate(split3(top + jnp.log2(total))):
            logs = jnp.where(line[:16] == 3 * h + part, piece, logs)
    shares = jnp.transpose(shares)[:rows]
    for h in range(heads):
        value = a[h * rows : (h + 1) * rows].astype(jnp.float32) * shares[:, 2 * h : 2 * h + 1]
        value = value + b[h * rows : (h + 1) * rows].astype(jnp.float32) * shares[:, 2 * h + 1 : 2 * h + 2]
        out_ref[h * rows : (h + 1) * rows] = value.astype(jnp.bfloat16)
    if not last:
        low = logs.astype(jnp.bfloat16)
        out_ref[at : at + 16] = low[:, :128]
        out_ref[at + 16 : at + 32] = low[:, 128:]


def merge_core_kernel(rows, heads, a_ref, b_ref, keep_ref, send_ref):
    merge_two(rows, heads, a_ref[1], b_ref[1], send_ref, False)
    merge_two(rows, heads, a_ref[0], b_ref[0], keep_ref, False)


def merge_far_kernel(rows, heads, a_ref, b_ref, out_ref):
    merge_two(rows, heads, a_ref[...], b_ref[...], out_ref, True)


def merge_core(keep, other, heads):
    _, lines, size = keep.shape
    out = jax.ShapeDtypeStruct((lines, size), jnp.bfloat16)
    return pl.pallas_call(
        functools.partial(merge_core_kernel, (lines - 32) // heads, heads),
        out_shape=(out, out),
        in_specs=[VMEM, VMEM],
        out_specs=(VMEM, VMEM),
        compiler_params=PARAMS,
        name="merge_core",
    )(keep, other)


def merge_far(keep, other, heads):
    lines, size = keep.shape
    return pl.pallas_call(
        functools.partial(merge_far_kernel, (lines - 32) // heads, heads),
        out_shape=jax.ShapeDtypeStruct((lines - 32, size), jnp.bfloat16),
        in_specs=[VMEM, VMEM],
        out_specs=VMEM,
        compiler_params=PARAMS,
        cost_estimate=pl.CostEstimate(flops=1 << 31, bytes_accessed=7 << 20, transcendentals=0),
        name="merge_far",
    )(keep, other)


def project_kernel(ring, idx_ref, att_ref, w0_ref, w1_ref, w2_ref, w3_ref, w4_ref, keep_ref, send_ref):
    y, c = idx_ref[0], idx_ref[2]
    cores, heads, rows, size = att_ref.shape
    deep = w0_ref.shape[1]
    line = lax.broadcasted_iota(jnp.int32, (size, size), 0)
    lane = lax.broadcasted_iota(jnp.int32, (size, size), 1)
    sources = [jnp.where(c == 0, (y + ring - hops) % ring, (y + hops) % ring) for hops in (1, 2, 3)]
    lefts, rights = [], []
    for h in range(0, heads, 2):
        opposite = h < heads // 2
        if h % (heads // 2) == 0:
            moves = []
            for side in range(2):
                wanted = jnp.full((size, size), -1, jnp.int32)
                for slot, source in enumerate([(y + 4) % ring if opposite else y] + sources):
                    at = side * size // 2 + slot * deep
                    inside = jnp.logical_and(lane >= at, lane < at + deep)
                    wanted = jnp.where(inside, lane + (source * deep - at), wanted)
                moves.append(jnp.where(line == wanted, 1.0, 0.0).astype(jnp.bfloat16))
        left = None
        for side in range(2):
            place = (h + side + jnp.where(c == 0, heads // 2, 0)) % heads
            columns = jnp.concatenate([att_ref[core, place] for core in range(cores)], axis=0)
            moved = jnp.dot(columns, moves[side], preferred_element_type=jnp.float32)
            left = moved if left is None else left + moved
            rights += [(ref, h + side) for ref in (w4_ref if opposite else w0_ref, w1_ref, w2_ref, w3_ref)]
        lefts.append(left.astype(jnp.bfloat16))
    left = jnp.concatenate(lefts, axis=1)
    for at in range(0, w0_ref.shape[2], 256):
        right = jnp.concatenate([ref[h, :, at : at + 256] for ref, h in rights], axis=0)
        total = jnp.dot(left, right, preferred_element_type=jnp.float32)
        first, second = total[:rows], total[rows:]
        keep_ref[:, at : at + 256] = jnp.where(c == 0, first, second)
        send_ref[:, at : at + 256] = jnp.where(c == 0, second, first).astype(jnp.bfloat16)


def project(idx, attended, weights, ring):
    _, _, rows, _ = attended.shape
    shape = (rows, weights[0].shape[2])
    return pl.pallas_call(
        functools.partial(project_kernel, ring),
        out_shape=(jax.ShapeDtypeStruct(shape, jnp.float32), jax.ShapeDtypeStruct(shape, jnp.bfloat16)),
        in_specs=[SMEM] + [VMEM] * (1 + len(weights)),
        out_specs=(VMEM, VMEM),
        compiler_params=PARAMS,
        name="project",
    )(idx, attended, *weights)


def join_kernel(keep_ref, other_ref, out_ref):
    out_ref[...] = (keep_ref[...] + other_ref[...].astype(jnp.float32)).astype(jnp.bfloat16)


def join(keep, other):
    return pl.pallas_call(
        join_kernel,
        out_shape=jax.ShapeDtypeStruct(other.shape, jnp.bfloat16),
        in_specs=[VMEM, VMEM],
        out_specs=VMEM,
        compiler_params=PARAMS,
        name="join",
    )(keep, other)


def finish_kernel(pieces_ref, bias_ref, out_ref):
    total = pieces_ref[0].astype(jnp.float32)
    for part in range(1, pieces_ref.shape[0]):
        total = total + pieces_ref[part].astype(jnp.float32)
    out_ref[...] = (total + bias_ref[...]).astype(jnp.bfloat16)


def finish(pieces, bias):
    return pl.pallas_call(
        finish_kernel,
        out_shape=jax.ShapeDtypeStruct(pieces.shape[1:], jnp.bfloat16),
        in_specs=[VMEM, VMEM],
        out_specs=VMEM,
        compiler_params=PARAMS,
        name="finish",
    )(pieces, bias)


def on_device(query_rows, key_rows, value_rows, out_weight, out_bias):
    rows, heads, size = query_rows.shape
    ring = lax.axis_size("y")
    y, zh, c = lax.axis_index("y"), lax.axis_index("zh"), lax.axis_index("c")
    idx = jnp.stack([y, zh, c]).astype(jnp.int32)

    def onward(block, hops):
        pairs = []
        for at in range(ring):
            pairs.append((2 * at, 2 * ((at + hops) % ring)))
            pairs.append((2 * at + 1, 2 * ((at - hops) % ring) + 1))
        return lax.ppermute(block, ("y", "c"), pairs)

    swap = [(0, 1), (1, 0)]

    own = jnp.stack([jnp.swapaxes(key_rows, 0, 1), jnp.swapaxes(value_rows, 0, 1)])
    chip = lax.all_gather(own, "c", axis=0)
    b2 = onward(chip, 2)
    query, weight, _ = lax.optimization_barrier((jnp.swapaxes(query_rows, 0, 1), out_weight, chip))
    qw = pack(query, weight)
    near_chip, qw = lax.optimization_barrier((chip, qw))
    b1 = onward(near_chip, 1)
    qw_far = lax.ppermute(qw, "zh", swap)
    qw_own = lax.all_gather(qw, "c", axis=0)
    qw_far = lax.all_gather(qw_far, "c", axis=0)
    b2, qw_own = lax.optimization_barrier((b2, qw_own))
    b3 = onward(b2, 1)
    b4 = onward(lax.dynamic_index_in_dim(b2, c, 0, keepdims=False), 2)
    query, weight = unpack(idx, qw_own, qw_far, heads, rows, out_weight.shape)
    state = attend_near(idx, query, own, b1, b2, ring)

    weight, state = lax.optimization_barrier((weight, state))
    w2 = onward(weight, 2)
    w1 = onward(weight, 1)
    keep, send = attend_far(idx, query, b3, b4, state, ring)
    keep, send = merge_core(keep, lax.ppermute(send, "c", swap), heads)
    other = lax.ppermute(send, "zh", swap)
    w3 = onward(w2, 1)
    w4 = onward(w2[: w2.shape[0] // 2], 2)
    attended = merge_far(keep, other, heads)
    attended = attended.reshape(heads, rows, size)
    attended = lax.all_gather(attended, "col", axis=0, tiled=True)
    attended = lax.all_gather(attended, "c", axis=0)
    keep, send = project(idx, attended, (weight, w1, w2, w3, w4), ring)
    joined = join(keep, lax.ppermute(send, "c", swap))
    parts = lax.axis_size("row")
    pieces = joined.reshape(parts, rows // parts, joined.shape[1])
    pieces = lax.all_to_all(pieces, "row", 0, 0, tiled=True)
    return finish(pieces, out_bias[None, :])


def solution(mesh):
    shape = mesh.devices.shape
    fine = Mesh(mesh.devices.reshape((shape[0] // 4, 2, 2) + shape[1:]), ("y", "zh", "c", "row", "col"))
    seq = ("y", "zh", "c")
    in_specs = (
        P(seq, ("row", "col"), None),
        P(seq, ("row", "col"), None),
        P(seq, ("row", "col"), None),
        P("row", seq, "col"),
        P("col"),
    )
    out_specs = P(seq + ("row",), "col")
    return jax.shard_map(
        on_device, mesh=fine, in_specs=in_specs, out_specs=out_specs, check_vma=False
    )
```

```python
import functools
import math

import jax
import jax.numpy as jnp
from jax import lax
from jax.experimental import pallas as pl
from jax.experimental.pallas import tpu as pltpu
from jax.sharding import Mesh
from jax.sharding import PartitionSpec as P

LOW = -1e30
VMEM = pl.BlockSpec(memory_space=pltpu.VMEM)
SMEM = pl.BlockSpec(memory_space=pltpu.SMEM)
ROOMY = pltpu.CompilerParams(vmem_limit_bytes=60 * 1024 * 1024)
PARAMS = pltpu.CompilerParams(vmem_limit_bytes=48 * 1024 * 1024)


def split3(x):
    high = x.astype(jnp.bfloat16).astype(jnp.float32)
    rest = x - high
    mid = rest.astype(jnp.bfloat16).astype(jnp.float32)
    return high, mid, rest - mid


def attend_block(state, scale2, query, keys, values, seen, allowed=None):
    scores = lax.dot_general(keys, query, (((1,), (1,)), ((), ())), preferred_element_type=jnp.float32)
    if allowed is not None:
        scores = jnp.where(allowed, scores, LOW)
    top = jnp.where(seen, jnp.max(scores, axis=0, keepdims=True) * scale2, LOW)
    new = top if state is None else jnp.maximum(state[0], top)
    shift = jnp.where(jnp.logical_and(new > 0.5 * LOW, seen), new, -LOW)
    weights = jnp.exp2(scores * scale2 - shift)
    total = jnp.sum(weights, axis=0, keepdims=True)
    sums = lax.dot_general(
        values, weights.astype(jnp.bfloat16), (((0,), (0,)), ((), ())), preferred_element_type=jnp.float32
    )
    if state is None:
        return new, total, sums
    fade = jnp.exp2(state[0] - new)
    return new, state[1] * fade + total, state[2] * fade + sums


def chip_block(ref, h):
    keys = jnp.concatenate([ref[0, 0, h], ref[1, 0, h]], axis=0)
    values = jnp.concatenate([ref[0, 1, h], ref[1, 1, h]], axis=0)
    return keys, values


def source_of(idx_ref, ring, distance):
    y, c = idx_ref[0], idx_ref[2]
    return jnp.where(c == 0, y + ring - distance, y + distance) % ring


def whole(shape):
    return pl.BlockSpec(shape, lambda i: (0,) * len(shape))


def pack_kernel(q_ref, w_ref, qw_ref):
    heads, rows, size = q_ref.shape
    for h in range(heads):
        qw_ref[h * rows : (h + 1) * rows] = q_ref[h]
    w_heads, deep, wide = w_ref.shape
    group, tiles = 16 // deep, wide // 128
    for g in range(w_heads // group):
        lines = jnp.concatenate([w_ref[g * group + k].astype(jnp.float32) for k in range(group)], axis=0)
        lines = lines.astype(jnp.bfloat16)
        for t in range(tiles):
            at = heads * rows + (g * tiles + t) * 16
            qw_ref[at : at + 16] = lines[:, t * 128 : (t + 1) * 128]


def pack(q, w):
    heads, rows, size = q.shape
    lines = heads * rows + math.prod(w.shape) // 128
    return pl.pallas_call(
        pack_kernel,
        out_shape=jax.ShapeDtypeStruct((lines, 128), jnp.bfloat16),
        grid=(1,),
        in_specs=[whole(q.shape), whole(w.shape)],
        out_specs=whole((lines, 128)),
        compiler_params=ROOMY,
        name="pack",
    )(q, w)


def unpack_kernel(heads, rows, deep, idx_ref, own_ref, far_ref, query_ref, w_ref):
    first = idx_ref[1] == 0
    w_heads, _, wide = w_ref.shape
    turn = jnp.where(idx_ref[2] == 0, w_heads // 2, 0)

    def lines(at, count):
        near = [own_ref[core, at : at + count] for core in range(2)]
        far = [far_ref[core, at : at + count] for core in range(2)]
        low = [jnp.where(first, a, b) for a, b in zip(near, far)]
        return low + [jnp.where(first, b, a) for a, b in zip(near, far)]

    for h in range(heads):
        for block, value in enumerate(lines(h * rows, rows)):
            query_ref[h, block * rows : (block + 1) * rows] = value
    group, tiles = 16 // deep, wide // 128
    for g in range(w_heads // group):
        for t in range(tiles):
            tile = [x.astype(jnp.float32) for x in lines(heads * rows + (g * tiles + t) * 16, 16)]
            for k in range(group):
                piece = jnp.concatenate([x[k * deep : (k + 1) * deep] for x in tile], axis=0).astype(jnp.bfloat16)
                w_ref[(g * group + k + turn) % w_heads, :, t * 128 : (t + 1) * 128] = piece


def unpack(idx, own, far, heads, rows, w_shape):
    w_heads, deep, wide = w_shape
    return pl.pallas_call(
        functools.partial(unpack_kernel, heads, rows, deep),
        out_shape=(
            jax.ShapeDtypeStruct((heads, 4 * rows, 128), jnp.bfloat16),
            jax.ShapeDtypeStruct((w_heads, 4 * deep, wide), jnp.bfloat16),
        ),
        in_specs=[SMEM, VMEM, VMEM],
        out_specs=(VMEM, VMEM),
        compiler_params=PARAMS,
        cost_estimate=pl.CostEstimate(flops=1 << 28, bytes_accessed=1 << 20, transcendentals=0),
        name="unpack",
    )(idx, own, far)


def near_kernel(rows, heads, ring, scale2, idx_ref, q_ref, own_ref, b1_ref, b2_ref, m_ref, l_ref, acc_ref):
    y, zh, c = idx_ref[0], idx_ref[1], idx_ref[2]
    query_pos = lax.broadcasted_iota(jnp.int32, (1, 4 * rows), 1)
    key_pos = (zh * 2 + c) * rows + lax.broadcasted_iota(jnp.int32, (rows, 1), 0)
    own_seen = query_pos >= (zh * 2 + c) * rows
    for h in range(heads):
        query = q_ref[h]
        state = attend_block(
            None, scale2, query, own_ref[0, h], own_ref[1, h], own_seen, key_pos <= query_pos
        )
        for distance, block_ref in ((1, b1_ref), (2, b2_ref)):
            seen = source_of(idx_ref, ring, distance) < y
            state = attend_block(state, scale2, query, *chip_block(block_ref, h), seen)
        m_ref[h], l_ref[h], acc_ref[h] = state


def far_kernel(rows, heads, ring, scale2, idx_ref, q_ref, b3_ref, b4_ref, m_ref, l_ref, acc_ref, keep_ref, send_ref):
    y, zh, c = idx_ref[0], idx_ref[1], idx_ref[2]

    def put(z, at, first, second):
        place = jnp.where(zh == z, 0, 1)
        keep_ref[place, at : at + first.shape[0]] = jnp.where(c == 0, first, second)
        send_ref[place, at : at + first.shape[0]] = jnp.where(c == 0, second, first)

    line = lax.broadcasted_iota(jnp.int32, (16, 4 * rows), 0)
    plane = jnp.zeros((16, 4 * rows), jnp.float32)
    for h in range(heads):
        query = q_ref[h]
        state = m_ref[h], l_ref[h], acc_ref[h]
        seen = source_of(idx_ref, ring, 4) < y
        state = attend_block(state, scale2, query, b4_ref[0, h], b4_ref[1, h], seen)
        seen = source_of(idx_ref, ring, 3) < y
        most, total, sums = attend_block(state, scale2, query, *chip_block(b3_ref, h), seen)
        seen = total > 0.0
        safe = jnp.where(seen, total, 1.0)
        low = jnp.transpose(sums * (1.0 / safe)).astype(jnp.bfloat16)
        for z in range(2):
            put(z, h * rows, low[2 * z * rows : (2 * z + 1) * rows], low[(2 * z + 1) * rows : (2 * z + 2) * rows])
        log = jnp.where(seen, most + jnp.log2(safe), LOW)
        for part, piece in enumerate(split3(log)):
            plane = jnp.where(line == 3 * h + part, piece, plane)
    plane = jnp.concatenate([plane, jnp.zeros((16, 128), jnp.float32)], axis=1)
    for z in range(2):
        first, second = [
            plane[:, block * rows : block * rows + 256].astype(jnp.bfloat16) for block in (2 * z, 2 * z + 1)
        ]
        put(z, heads * rows, first[:, :128], second[:, :128])
        put(z, heads * rows + 16, first[:, 128:], second[:, 128:])


def state_shapes(heads, rows, size, kind):
    return (
        kind((heads, 1, 4 * rows), jnp.float32),
        kind((heads, 1, 4 * rows), jnp.float32),
        kind((heads, size, 4 * rows), jnp.float32),
    )


def attend_near(idx, query, own, b1, b2, ring):
    heads, rows, size = query.shape[0], query.shape[1] // 4, query.shape[2]
    scale2 = size ** (-0.5) * math.log2(math.e)
    keys = 5 * rows
    return pl.pallas_call(
        functools.partial(near_kernel, rows, heads, ring, scale2),
        out_shape=state_shapes(heads, rows, size, jax.ShapeDtypeStruct),
        in_specs=[SMEM] + [VMEM] * 4,
        out_specs=(VMEM,) * 3,
        compiler_params=PARAMS,
        cost_estimate=pl.CostEstimate(flops=1 << 28, bytes_accessed=1 << 18, transcendentals=0),
        name="attend_near",
    )(idx, query, own, b1, b2)


def attend_far(idx, query, b3, b4, state, ring):
    heads, rows, size = query.shape[0], query.shape[1] // 4, query.shape[2]
    scale2 = size ** (-0.5) * math.log2(math.e)
    out = jax.ShapeDtypeStruct((2, heads * rows + 32, size), jnp.bfloat16)
    keys = 3 * rows
    return pl.pallas_call(
        functools.partial(far_kernel, rows, heads, ring, scale2),
        out_shape=(out, out),
        in_specs=[SMEM] + [VMEM] * 6,
        out_specs=(VMEM, VMEM),
        compiler_params=PARAMS,
        cost_estimate=pl.CostEstimate(flops=1 << 31, bytes_accessed=1 << 18, transcendentals=0),
        name="attend_far",
    )(idx, query, b3, b4, *state)


def merge_two(rows, heads, a, b, out_ref, last):
    at = heads * rows
    planes = [jnp.concatenate([x[at : at + 16], x[at + 16 : at + 32]], axis=1).astype(jnp.float32) for x in (a, b)]
    line = lax.broadcasted_iota(jnp.int32, (128, 256), 0)
    shares = jnp.zeros((128, 256), jnp.float32)
    logs = jnp.zeros((16, 256), jnp.float32)
    for h in range(heads):
        log_a, log_b = [p[3 * h : 3 * h + 1] + p[3 * h + 1 : 3 * h + 2] + p[3 * h + 2 : 3 * h + 3] for p in planes]
        top = jnp.maximum(log_a, log_b)
        part_a, part_b = jnp.exp2(log_a - top), jnp.exp2(log_b - top)
        total = part_a + part_b
        shares = jnp.where(line == 2 * h, part_a / total, shares)
        shares = jnp.where(line == 2 * h + 1, part_b / total, shares)
        for part, piece in enumerate(split3(top + jnp.log2(total))):
            logs = jnp.where(line[:16] == 3 * h + part, piece, logs)
    shares = jnp.transpose(shares)[:rows]
    for h in range(heads):
        value = a[h * rows : (h + 1) * rows].astype(jnp.float32) * shares[:, 2 * h : 2 * h + 1]
        value = value + b[h * rows : (h + 1) * rows].astype(jnp.float32) * shares[:, 2 * h + 1 : 2 * h + 2]
        out_ref[h * rows : (h + 1) * rows] = value.astype(jnp.bfloat16)
    if not last:
        low = logs.astype(jnp.bfloat16)
        out_ref[at : at + 16] = low[:, :128]
        out_ref[at + 16 : at + 32] = low[:, 128:]


def merge_core_kernel(rows, heads, idx_ref, a_ref, b_ref, keep_ref, send_ref):
    other = 1 - idx_ref[2]
    merge_two(rows, heads, a_ref[1], b_ref[other, 1], send_ref, False)
    merge_two(rows, heads, a_ref[0], b_ref[other, 0], keep_ref, False)


def merge_far_kernel(rows, heads, a_ref, b_ref, out_ref):
    merge_two(rows, heads, a_ref[...], b_ref[...], out_ref, True)


def merge_core(idx, keep, both, heads):
    _, lines, size = keep.shape
    out = jax.ShapeDtypeStruct((lines, size), jnp.bfloat16)
    return pl.pallas_call(
        functools.partial(merge_core_kernel, (lines - 32) // heads, heads),
        out_shape=(out, out),
        in_specs=[SMEM, VMEM, VMEM],
        out_specs=(VMEM, VMEM),
        compiler_params=PARAMS,
        name="merge_core",
    )(idx, keep, both)


def merge_far(keep, other, heads):
    lines, size = keep.shape
    return pl.pallas_call(
        functools.partial(merge_far_kernel, (lines - 32) // heads, heads),
        out_shape=jax.ShapeDtypeStruct((lines - 32, size), jnp.bfloat16),
        in_specs=[VMEM, VMEM],
        out_specs=VMEM,
        compiler_params=PARAMS,
        cost_estimate=pl.CostEstimate(flops=1 << 31, bytes_accessed=7 << 20, transcendentals=0),
        name="merge_far",
    )(keep, other)


def project_kernel(ring, idx_ref, att_ref, w0_ref, w1_ref, w2_ref, w3_ref, w4_ref, keep_ref, send_ref):
    y, c = idx_ref[0], idx_ref[2]
    cores, heads, rows, size = att_ref.shape
    deep = w0_ref.shape[1]
    line = lax.broadcasted_iota(jnp.int32, (size, size), 0)
    lane = lax.broadcasted_iota(jnp.int32, (size, size), 1)
    sources = [jnp.where(c == 0, (y + ring - hops) % ring, (y + hops) % ring) for hops in (1, 2, 3)]
    lefts, rights = [], []
    for h in range(0, heads, 2):
        opposite = h < heads // 2
        if h % (heads // 2) == 0:
            moves = []
            for side in range(2):
                wanted = jnp.full((size, size), -1, jnp.int32)
                for slot, source in enumerate([(y + 4) % ring if opposite else y] + sources):
                    at = side * size // 2 + slot * deep
                    inside = jnp.logical_and(lane >= at, lane < at + deep)
                    wanted = jnp.where(inside, lane + (source * deep - at), wanted)
                moves.append(jnp.where(line == wanted, 1.0, 0.0).astype(jnp.bfloat16))
        left = None
        for side in range(2):
            place = (h + side + jnp.where(c == 0, heads // 2, 0)) % heads
            columns = jnp.concatenate([att_ref[core, place] for core in range(cores)], axis=0)
            moved = jnp.dot(columns, moves[side], preferred_element_type=jnp.float32)
            left = moved if left is None else left + moved
            rights += [(ref, h + side) for ref in (w4_ref if opposite else w0_ref, w1_ref, w2_ref, w3_ref)]
        lefts.append(left.astype(jnp.bfloat16))
    left = jnp.concatenate(lefts, axis=1)
    for at in range(0, w0_ref.shape[2], 256):
        right = jnp.concatenate([ref[h, :, at : at + 256] for ref, h in rights], axis=0)
        total = jnp.dot(left, right, preferred_element_type=jnp.float32)
        first, second = total[:rows], total[rows:]
        keep_ref[:, at : at + 256] = jnp.where(c == 0, first, second)
        send_ref[:, at : at + 256] = jnp.where(c == 0, second, first).astype(jnp.bfloat16)


def project(idx, attended, weights, ring):
    _, _, rows, _ = attended.shape
    shape = (rows, weights[0].shape[2])
    return pl.pallas_call(
        functools.partial(project_kernel, ring),
        out_shape=(jax.ShapeDtypeStruct(shape, jnp.float32), jax.ShapeDtypeStruct(shape, jnp.bfloat16)),
        in_specs=[SMEM] + [VMEM] * (1 + len(weights)),
        out_specs=(VMEM, VMEM),
        compiler_params=PARAMS,
        name="project",
    )(idx, attended, *weights)


def join_kernel(idx_ref, keep_ref, both_ref, out_ref):
    out_ref[...] = (keep_ref[...] + both_ref[1 - idx_ref[2]].astype(jnp.float32)).astype(jnp.bfloat16)


def join(idx, keep, both):
    return pl.pallas_call(
        join_kernel,
        out_shape=jax.ShapeDtypeStruct(both.shape[1:], jnp.bfloat16),
        in_specs=[SMEM, VMEM, VMEM],
        out_specs=VMEM,
        compiler_params=PARAMS,
        name="join",
    )(idx, keep, both)


def finish_kernel(pieces_ref, bias_ref, out_ref):
    total = pieces_ref[0].astype(jnp.float32)
    for part in range(1, pieces_ref.shape[0]):
        total = total + pieces_ref[part].astype(jnp.float32)
    out_ref[...] = (total + bias_ref[...]).astype(jnp.bfloat16)


def finish(pieces, bias):
    return pl.pallas_call(
        finish_kernel,
        out_shape=jax.ShapeDtypeStruct(pieces.shape[1:], jnp.bfloat16),
        in_specs=[VMEM, VMEM],
        out_specs=VMEM,
        compiler_params=PARAMS,
        name="finish",
    )(pieces, bias)


def on_device(query_rows, key_rows, value_rows, out_weight, out_bias):
    rows, heads, size = query_rows.shape
    ring = lax.axis_size("y")
    y, zh, c = lax.axis_index("y"), lax.axis_index("zh"), lax.axis_index("c")
    idx = jnp.stack([y, zh, c]).astype(jnp.int32)

    def onward(block, hops):
        pairs = []
        for at in range(ring):
            pairs.append((2 * at, 2 * ((at + hops) % ring)))
            pairs.append((2 * at + 1, 2 * ((at - hops) % ring) + 1))
        return lax.ppermute(block, ("y", "c"), pairs)

    swap = [(0, 1), (1, 0)]

    own = jnp.stack([jnp.swapaxes(key_rows, 0, 1), jnp.swapaxes(value_rows, 0, 1)])
    chip = lax.all_gather(own, "c", axis=0)
    b2 = onward(chip, 2)
    query, weight, _ = lax.optimization_barrier((jnp.swapaxes(query_rows, 0, 1), out_weight, chip))
    qw = pack(query, weight)
    near_chip, qw = lax.optimization_barrier((chip, qw))
    b1 = onward(near_chip, 1)
    qw_far = lax.ppermute(qw, "zh", swap)
    qw_own = lax.all_gather(qw, "c", axis=0)
    qw_far = lax.all_gather(qw_far, "c", axis=0)
    b2, qw_own = lax.optimization_barrier((b2, qw_own))
    b3 = onward(b2, 1)
    b4 = onward(lax.dynamic_index_in_dim(b2, c, 0, keepdims=False), 2)
    query, weight = unpack(idx, qw_own, qw_far, heads, rows, out_weight.shape)
    state = attend_near(idx, query, own, b1, b2, ring)

    weight, state = lax.optimization_barrier((weight, state))
    w2 = onward(weight, 2)
    w1 = onward(weight, 1)
    keep, send = attend_far(idx, query, b3, b4, state, ring)
    keep, send = merge_core(idx, keep, lax.all_gather(send, "c", axis=0), heads)
    other = lax.ppermute(send, "zh", swap)
    w3 = onward(w2, 1)
    w4 = onward(w2[: w2.shape[0] // 2], 2)
    attended = merge_far(keep, other, heads)
    attended = attended.reshape(heads, rows, size)
    attended = lax.all_gather(attended, "col", axis=0, tiled=True)
    attended = lax.all_gather(attended, "c", axis=0)
    keep, send = project(idx, attended, (weight, w1, w2, w3, w4), ring)
    joined = join(idx, keep, lax.all_gather(send, "c", axis=0))
    parts = lax.axis_size("row")
    pieces = joined.reshape(parts, rows // parts, joined.shape[1])
    pieces = lax.all_to_all(pieces, "row", 0, 0, tiled=True)
    return finish(pieces, out_bias[None, :])


def solution(mesh):
    shape = mesh.devices.shape
    fine = Mesh(mesh.devices.reshape((shape[0] // 4, 2, 2) + shape[1:]), ("y", "zh", "c", "row", "col"))
    seq = ("y", "zh", "c")
    in_specs = (
        P(seq, ("row", "col"), None),
        P(seq, ("row", "col"), None),
        P(seq, ("row", "col"), None),
        P("row", seq, "col"),
        P("col"),
    )
    out_specs = P(seq + ("row",), "col")
    return jax.shard_map(
        on_device, mesh=fine, in_specs=in_specs, out_specs=out_specs, check_vma=False
    )
```

```python
import functools
import math

import jax
import jax.numpy as jnp
from jax import lax
from jax.experimental import pallas as pl
from jax.experimental.pallas import tpu as pltpu
from jax.sharding import Mesh
from jax.sharding import PartitionSpec as P

LOW = -1e30
VMEM = pl.BlockSpec(memory_space=pltpu.VMEM)
SMEM = pl.BlockSpec(memory_space=pltpu.SMEM)
ROOMY = pltpu.CompilerParams(vmem_limit_bytes=60 * 1024 * 1024)
PARAMS = pltpu.CompilerParams(vmem_limit_bytes=48 * 1024 * 1024)


def split3(x):
    high = x.astype(jnp.bfloat16).astype(jnp.float32)
    rest = x - high
    mid = rest.astype(jnp.bfloat16).astype(jnp.float32)
    return high, mid, rest - mid


def attend_block(state, scale2, query, keys, values, seen, allowed=None):
    scores = lax.dot_general(keys, query, (((1,), (1,)), ((), ())), preferred_element_type=jnp.float32)
    if allowed is not None:
        scores = jnp.where(allowed, scores, LOW)
    top = jnp.where(seen, jnp.max(scores, axis=0, keepdims=True) * scale2, LOW)
    new = top if state is None else jnp.maximum(state[0], top)
    shift = jnp.where(jnp.logical_and(new > 0.5 * LOW, seen), new, -LOW)
    weights = jnp.exp2(scores * scale2 - shift)
    total = jnp.sum(weights, axis=0, keepdims=True)
    sums = lax.dot_general(
        values, weights.astype(jnp.bfloat16), (((0,), (0,)), ((), ())), preferred_element_type=jnp.float32
    )
    if state is None:
        return new, total, sums
    fade = jnp.exp2(state[0] - new)
    return new, state[1] * fade + total, state[2] * fade + sums


def chip_block(ref, h):
    keys = jnp.concatenate([ref[0, 0, h], ref[1, 0, h]], axis=0)
    values = jnp.concatenate([ref[0, 1, h], ref[1, 1, h]], axis=0)
    return keys, values


def source_of(idx_ref, ring, distance):
    y, c = idx_ref[0], idx_ref[2]
    return jnp.where(c == 0, y + ring - distance, y + distance) % ring


def whole(shape):
    return pl.BlockSpec(shape, lambda i: (0,) * len(shape))


def pack_kernel(q_ref, w_ref, qw_ref):
    heads, rows, size = q_ref.shape
    for h in range(heads):
        qw_ref[h * rows : (h + 1) * rows] = q_ref[h]
    w_heads, deep, wide = w_ref.shape
    group, tiles = 16 // deep, wide // 128
    for g in range(w_heads // group):
        lines = jnp.concatenate([w_ref[g * group + k].astype(jnp.float32) for k in range(group)], axis=0)
        lines = lines.astype(jnp.bfloat16)
        for t in range(tiles):
            at = heads * rows + (g * tiles + t) * 16
            qw_ref[at : at + 16] = lines[:, t * 128 : (t + 1) * 128]


def pack(q, w):
    heads, rows, size = q.shape
    lines = heads * rows + math.prod(w.shape) // 128
    return pl.pallas_call(
        pack_kernel,
        out_shape=jax.ShapeDtypeStruct((lines, 128), jnp.bfloat16),
        grid=(1,),
        in_specs=[whole(q.shape), whole(w.shape)],
        out_specs=whole((lines, 128)),
        compiler_params=ROOMY,
        name="pack",
    )(q, w)


def unpack_kernel(heads, rows, deep, idx_ref, own_ref, far_ref, query_ref, w_ref):
    first = idx_ref[1] == 0
    w_heads, _, wide = w_ref.shape
    turn = jnp.where(idx_ref[2] == 0, w_heads // 2, 0)

    def lines(at, count):
        near = [own_ref[core, at : at + count] for core in range(2)]
        far = [far_ref[core, at : at + count] for core in range(2)]
        low = [jnp.where(first, a, b) for a, b in zip(near, far)]
        return low + [jnp.where(first, b, a) for a, b in zip(near, far)]

    for h in range(heads):
        for block, value in enumerate(lines(h * rows, rows)):
            query_ref[h, block * rows : (block + 1) * rows] = value
    group, tiles = 16 // deep, wide // 128
    for g in range(w_heads // group):
        for t in range(tiles):
            tile = [x.astype(jnp.float32) for x in lines(heads * rows + (g * tiles + t) * 16, 16)]
            for k in range(group):
                piece = jnp.concatenate([x[k * deep : (k + 1) * deep] for x in tile], axis=0).astype(jnp.bfloat16)
                w_ref[(g * group + k + turn) % w_heads, :, t * 128 : (t + 1) * 128] = piece


def unpack(idx, own, far, heads, rows, w_shape):
    w_heads, deep, wide = w_shape
    return pl.pallas_call(
        functools.partial(unpack_kernel, heads, rows, deep),
        out_shape=(
            jax.ShapeDtypeStruct((heads, 4 * rows, 128), jnp.bfloat16),
            jax.ShapeDtypeStruct((w_heads, 4 * deep, wide), jnp.bfloat16),
        ),
        in_specs=[SMEM, VMEM, VMEM],
        out_specs=(VMEM, VMEM),
        compiler_params=PARAMS,
        cost_estimate=pl.CostEstimate(flops=1 << 28, bytes_accessed=1 << 20, transcendentals=0),
        name="unpack",
    )(idx, own, far)


def near_kernel(rows, heads, ring, scale2, idx_ref, q_ref, own_ref, b1_ref, b2_ref, m_ref, l_ref, acc_ref):
    y, zh, c = idx_ref[0], idx_ref[1], idx_ref[2]
    query_pos = lax.broadcasted_iota(jnp.int32, (1, 4 * rows), 1)
    key_pos = (zh * 2 + c) * rows + lax.broadcasted_iota(jnp.int32, (rows, 1), 0)
    own_seen = query_pos >= (zh * 2 + c) * rows
    for h in range(heads):
        query = q_ref[h]
        state = attend_block(
            None, scale2, query, own_ref[0, h], own_ref[1, h], own_seen, key_pos <= query_pos
        )
        for distance, block_ref in ((1, b1_ref), (2, b2_ref)):
            seen = source_of(idx_ref, ring, distance) < y
            state = attend_block(state, scale2, query, *chip_block(block_ref, h), seen)
        m_ref[h], l_ref[h], acc_ref[h] = state


def far_kernel(rows, heads, ring, scale2, idx_ref, q_ref, b3_ref, b4_ref, m_ref, l_ref, acc_ref, keep_ref, send_ref):
    y, zh, c = idx_ref[0], idx_ref[1], idx_ref[2]

    def put(z, at, first, second):
        place = jnp.where(zh == z, 0, 1)
        keep_ref[place, at : at + first.shape[0]] = jnp.where(c == 0, first, second)
        send_ref[place, at : at + first.shape[0]] = jnp.where(c == 0, second, first)

    line = lax.broadcasted_iota(jnp.int32, (16, 4 * rows), 0)
    plane = jnp.zeros((16, 4 * rows), jnp.float32)
    for h in range(heads):
        query = q_ref[h]
        state = m_ref[h], l_ref[h], acc_ref[h]
        seen = source_of(idx_ref, ring, 4) < y
        state = attend_block(state, scale2, query, b4_ref[0, h], b4_ref[1, h], seen)
        seen = source_of(idx_ref, ring, 3) < y
        most, total, sums = attend_block(state, scale2, query, *chip_block(b3_ref, h), seen)
        seen = total > 0.0
        safe = jnp.where(seen, total, 1.0)
        low = jnp.transpose(sums * (1.0 / safe)).astype(jnp.bfloat16)
        for z in range(2):
            put(z, h * rows, low[2 * z * rows : (2 * z + 1) * rows], low[(2 * z + 1) * rows : (2 * z + 2) * rows])
        log = jnp.where(seen, most + jnp.log2(safe), LOW)
        for part, piece in enumerate(split3(log)):
            plane = jnp.where(line == 3 * h + part, piece, plane)
    plane = jnp.concatenate([plane, jnp.zeros((16, 128), jnp.float32)], axis=1)
    for z in range(2):
        first, second = [
            plane[:, block * rows : block * rows + 256].astype(jnp.bfloat16) for block in (2 * z, 2 * z + 1)
        ]
        put(z, heads * rows, first[:, :128], second[:, :128])
        put(z, heads * rows + 16, first[:, 128:], second[:, 128:])


def state_shapes(heads, rows, size, kind):
    return (
        kind((heads, 1, 4 * rows), jnp.float32),
        kind((heads, 1, 4 * rows), jnp.float32),
        kind((heads, size, 4 * rows), jnp.float32),
    )


def attend_near(idx, query, own, b1, b2, ring):
    heads, rows, size = query.shape[0], query.shape[1] // 4, query.shape[2]
    scale2 = size ** (-0.5) * math.log2(math.e)
    keys = 5 * rows
    return pl.pallas_call(
        functools.partial(near_kernel, rows, heads, ring, scale2),
        out_shape=state_shapes(heads, rows, size, jax.ShapeDtypeStruct),
        in_specs=[SMEM] + [VMEM] * 4,
        out_specs=(VMEM,) * 3,
        compiler_params=PARAMS,
        cost_estimate=pl.CostEstimate(flops=1 << 28, bytes_accessed=1 << 18, transcendentals=0),
        name="attend_near",
    )(idx, query, own, b1, b2)


def attend_far(idx, query, b3, b4, state, ring):
    heads, rows, size = query.shape[0], query.shape[1] // 4, query.shape[2]
    scale2 = size ** (-0.5) * math.log2(math.e)
    out = jax.ShapeDtypeStruct((2, heads * rows + 32, size), jnp.bfloat16)
    keys = 3 * rows
    return pl.pallas_call(
        functools.partial(far_kernel, rows, heads, ring, scale2),
        out_shape=(out, out),
        in_specs=[SMEM] + [VMEM] * 6,
        out_specs=(VMEM, VMEM),
        compiler_params=PARAMS,
        cost_estimate=pl.CostEstimate(flops=1 << 31, bytes_accessed=1 << 18, transcendentals=0),
        name="attend_far",
    )(idx, query, b3, b4, *state)


def merge_two(rows, heads, a, b, out_ref, last):
    at = heads * rows
    planes = [jnp.concatenate([x[at : at + 16], x[at + 16 : at + 32]], axis=1).astype(jnp.float32) for x in (a, b)]
    line = lax.broadcasted_iota(jnp.int32, (128, 256), 0)
    shares = jnp.zeros((128, 256), jnp.float32)
    logs = jnp.zeros((16, 256), jnp.float32)
    for h in range(heads):
        log_a, log_b = [p[3 * h : 3 * h + 1] + p[3 * h + 1 : 3 * h + 2] + p[3 * h + 2 : 3 * h + 3] for p in planes]
        top = jnp.maximum(log_a, log_b)
        part_a, part_b = jnp.exp2(log_a - top), jnp.exp2(log_b - top)
        total = part_a + part_b
        shares = jnp.where(line == 2 * h, part_a / total, shares)
        shares = jnp.where(line == 2 * h + 1, part_b / total, shares)
        for part, piece in enumerate(split3(top + jnp.log2(total))):
            logs = jnp.where(line[:16] == 3 * h + part, piece, logs)
    shares = jnp.transpose(shares)[:rows]
    for h in range(heads):
        value = a[h * rows : (h + 1) * rows].astype(jnp.float32) * shares[:, 2 * h : 2 * h + 1]
        value = value + b[h * rows : (h + 1) * rows].astype(jnp.float32) * shares[:, 2 * h + 1 : 2 * h + 2]
        out_ref[h * rows : (h + 1) * rows] = value.astype(jnp.bfloat16)
    if not last:
        low = logs.astype(jnp.bfloat16)
        out_ref[at : at + 16] = low[:, :128]
        out_ref[at + 16 : at + 32] = low[:, 128:]


def merge_core_kernel(rows, heads, idx_ref, a_ref, b_ref, keep_ref, send_ref):
    other = 1 - idx_ref[2]
    merge_two(rows, heads, a_ref[1], b_ref[other, 1], send_ref, False)
    merge_two(rows, heads, a_ref[0], b_ref[other, 0], keep_ref, False)


def merge_far_kernel(rows, heads, a_ref, b_ref, out_ref):
    merge_two(rows, heads, a_ref[...], b_ref[...], out_ref, True)


def merge_core(idx, keep, both, heads):
    _, lines, size = keep.shape
    out = jax.ShapeDtypeStruct((lines, size), jnp.bfloat16)
    return pl.pallas_call(
        functools.partial(merge_core_kernel, (lines - 32) // heads, heads),
        out_shape=(out, out),
        in_specs=[SMEM, VMEM, VMEM],
        out_specs=(VMEM, VMEM),
        compiler_params=PARAMS,
        name="merge_core",
    )(idx, keep, both)


def merge_far(keep, other, heads):
    lines, size = keep.shape
    return pl.pallas_call(
        functools.partial(merge_far_kernel, (lines - 32) // heads, heads),
        out_shape=jax.ShapeDtypeStruct((lines - 32, size), jnp.bfloat16),
        in_specs=[VMEM, VMEM],
        out_specs=VMEM,
        compiler_params=PARAMS,
        cost_estimate=pl.CostEstimate(flops=1 << 31, bytes_accessed=7 << 20, transcendentals=0),
        name="merge_far",
    )(keep, other)


def project_kernel(ring, idx_ref, att_ref, w0_ref, w1_ref, w2_ref, w3_ref, w4_ref, keep_ref, send_ref):
    y, c = idx_ref[0], idx_ref[2]
    cores, heads, rows, size = att_ref.shape
    deep = w0_ref.shape[1]
    line = lax.broadcasted_iota(jnp.int32, (size, size), 0)
    lane = lax.broadcasted_iota(jnp.int32, (size, size), 1)
    sources = [jnp.where(c == 0, (y + ring - hops) % ring, (y + hops) % ring) for hops in (1, 2, 3)]
    lefts, rights = [], []
    for h in range(0, heads, 2):
        opposite = h < heads // 2
        if h % (heads // 2) == 0:
            moves = []
            for side in range(2):
                wanted = jnp.full((size, size), -1, jnp.int32)
                for slot, source in enumerate([(y + 4) % ring if opposite else y] + sources):
                    at = side * size // 2 + slot * deep
                    inside = jnp.logical_and(lane >= at, lane < at + deep)
                    wanted = jnp.where(inside, lane + (source * deep - at), wanted)
                moves.append(jnp.where(line == wanted, 1.0, 0.0).astype(jnp.bfloat16))
        left = None
        for side in range(2):
            place = (h + side + jnp.where(c == 0, heads // 2, 0)) % heads
            columns = jnp.concatenate([att_ref[core, place] for core in range(cores)], axis=0)
            moved = jnp.dot(columns, moves[side], preferred_element_type=jnp.float32)
            left = moved if left is None else left + moved
            rights += [(ref, h + side) for ref in (w4_ref if opposite else w0_ref, w1_ref, w2_ref, w3_ref)]
        lefts.append(left.astype(jnp.bfloat16))
    left = jnp.concatenate(lefts, axis=1)
    for at in range(0, w0_ref.shape[2], 512):
        right = jnp.concatenate([ref[h, :, at : at + 512] for ref, h in rights], axis=0)
        total = jnp.dot(left, right, preferred_element_type=jnp.float32)
        first, second = total[:rows], total[rows:]
        keep_ref[:, at : at + 512] = jnp.where(c == 0, first, second).astype(jnp.bfloat16)
        send_ref[:, at : at + 512] = jnp.where(c == 0, second, first).astype(jnp.bfloat16)


def project(idx, attended, weights, ring):
    _, _, rows, _ = attended.shape
    shape = (rows, weights[0].shape[2])
    return pl.pallas_call(
        functools.partial(project_kernel, ring),
        out_shape=(jax.ShapeDtypeStruct(shape, jnp.bfloat16), jax.ShapeDtypeStruct(shape, jnp.bfloat16)),
        in_specs=[SMEM] + [VMEM] * (1 + len(weights)),
        out_specs=(VMEM, VMEM),
        compiler_params=PARAMS,
        name="project",
    )(idx, attended, *weights)


def join_kernel(idx_ref, keep_ref, both_ref, out_ref):
    out_ref[...] = (keep_ref[...].astype(jnp.float32) + both_ref[1 - idx_ref[2]].astype(jnp.float32)).astype(jnp.bfloat16)


def join(idx, keep, both):
    return pl.pallas_call(
        join_kernel,
        out_shape=jax.ShapeDtypeStruct(both.shape[1:], jnp.bfloat16),
        in_specs=[SMEM, VMEM, VMEM],
        out_specs=VMEM,
        compiler_params=PARAMS,
        name="join",
    )(idx, keep, both)


def finish_kernel(pieces_ref, bias_ref, out_ref):
    total = pieces_ref[0].astype(jnp.float32)
    for part in range(1, pieces_ref.shape[0]):
        total = total + pieces_ref[part].astype(jnp.float32)
    out_ref[...] = (total + bias_ref[...]).astype(jnp.bfloat16)


def finish(pieces, bias):
    return pl.pallas_call(
        finish_kernel,
        out_shape=jax.ShapeDtypeStruct(pieces.shape[1:], jnp.bfloat16),
        in_specs=[VMEM, VMEM],
        out_specs=VMEM,
        compiler_params=PARAMS,
        name="finish",
    )(pieces, bias)


def on_device(query_rows, key_rows, value_rows, out_weight, out_bias):
    rows, heads, size = query_rows.shape
    ring = lax.axis_size("y")
    y, zh, c = lax.axis_index("y"), lax.axis_index("zh"), lax.axis_index("c")
    idx = jnp.stack([y, zh, c]).astype(jnp.int32)

    def onward(block, hops):
        pairs = []
        for at in range(ring):
            pairs.append((2 * at, 2 * ((at + hops) % ring)))
            pairs.append((2 * at + 1, 2 * ((at - hops) % ring) + 1))
        return lax.ppermute(block, ("y", "c"), pairs)

    swap = [(0, 1), (1, 0)]

    own = jnp.stack([jnp.swapaxes(key_rows, 0, 1), jnp.swapaxes(value_rows, 0, 1)])
    chip = lax.all_gather(own, "c", axis=0)
    b2 = onward(chip, 2)
    query, weight, _ = lax.optimization_barrier((jnp.swapaxes(query_rows, 0, 1), out_weight, chip))
    qw = pack(query, weight)
    near_chip, qw = lax.optimization_barrier((chip, qw))
    b1 = onward(near_chip, 1)
    qw_far = lax.ppermute(qw, "zh", swap)
    qw_own = lax.all_gather(qw, "c", axis=0)
    qw_far = lax.all_gather(qw_far, "c", axis=0)
    b2, qw_own = lax.optimization_barrier((b2, qw_own))
    b3 = onward(b2, 1)
    b4 = onward(lax.dynamic_index_in_dim(b2, c, 0, keepdims=False), 2)
    query, weight = unpack(idx, qw_own, qw_far, heads, rows, out_weight.shape)
    state = attend_near(idx, query, own, b1, b2, ring)

    weight, state = lax.optimization_barrier((weight, state))
    w2 = onward(weight, 2)
    w1 = onward(weight, 1)
    keep, send = attend_far(idx, query, b3, b4, state, ring)
    keep, send = merge_core(idx, keep, lax.all_gather(send, "c", axis=0), heads)
    other = lax.ppermute(send, "zh", swap)
    w3 = onward(w2, 1)
    w4 = onward(w2[: w2.shape[0] // 2], 2)
    attended = merge_far(keep, other, heads)
    attended = attended.reshape(heads, rows, size)
    attended = lax.all_gather(attended, "col", axis=0, tiled=True)
    attended = lax.all_gather(attended, "c", axis=0)
    keep, send = project(idx, attended, (weight, w1, w2, w3, w4), ring)
    joined = join(idx, keep, lax.all_gather(send, "c", axis=0))
    parts = lax.axis_size("row")
    pieces = joined.reshape(parts, rows // parts, joined.shape[1])
    pieces = lax.all_to_all(pieces, "row", 0, 0, tiled=True)
    return finish(pieces, out_bias[None, :])


def solution(mesh):
    shape = mesh.devices.shape
    fine = Mesh(mesh.devices.reshape((shape[0] // 4, 2, 2) + shape[1:]), ("y", "zh", "c", "row", "col"))
    seq = ("y", "zh", "c")
    in_specs = (
        P(seq, ("row", "col"), None),
        P(seq, ("row", "col"), None),
        P(seq, ("row", "col"), None),
        P("row", seq, "col"),
        P("col"),
    )
    out_specs = P(seq + ("row",), "col")
    return jax.shard_map(
        on_device, mesh=fine, in_specs=in_specs, out_specs=out_specs, check_vma=False
    )
```

```python
import functools
import math

import jax
import jax.numpy as jnp
from jax import lax
from jax.experimental import pallas as pl
from jax.experimental.pallas import tpu as pltpu
from jax.sharding import Mesh
from jax.sharding import PartitionSpec as P

LOW = -1e30
VMEM = pl.BlockSpec(memory_space=pltpu.VMEM)
SMEM = pl.BlockSpec(memory_space=pltpu.SMEM)
ROOMY = pltpu.CompilerParams(vmem_limit_bytes=60 * 1024 * 1024)
PARAMS = pltpu.CompilerParams(vmem_limit_bytes=48 * 1024 * 1024)


def split3(x):
    high = x.astype(jnp.bfloat16).astype(jnp.float32)
    rest = x - high
    mid = rest.astype(jnp.bfloat16).astype(jnp.float32)
    return high, mid, rest - mid


def attend_block(state, scale2, query, keys, values, seen, allowed=None):
    scores = lax.dot_general(keys, query, (((1,), (1,)), ((), ())), preferred_element_type=jnp.float32)
    if allowed is not None:
        scores = jnp.where(allowed, scores, LOW)
    top = jnp.where(seen, jnp.max(scores, axis=0, keepdims=True) * scale2, LOW)
    new = top if state is None else jnp.maximum(state[0], top)
    shift = jnp.where(jnp.logical_and(new > 0.5 * LOW, seen), new, -LOW)
    weights = jnp.exp2(scores * scale2 - shift)
    total = jnp.sum(weights, axis=0, keepdims=True)
    sums = lax.dot_general(
        values, weights.astype(jnp.bfloat16), (((0,), (0,)), ((), ())), preferred_element_type=jnp.float32
    )
    if state is None:
        return new, total, sums
    fade = jnp.exp2(state[0] - new)
    return new, state[1] * fade + total, state[2] * fade + sums


def chip_block(ref, h):
    keys = jnp.concatenate([ref[0, 0, h], ref[1, 0, h]], axis=0)
    values = jnp.concatenate([ref[0, 1, h], ref[1, 1, h]], axis=0)
    return keys, values


def source_of(idx_ref, ring, distance):
    y, c = idx_ref[0], idx_ref[2]
    return jnp.where(c == 0, y + ring - distance, y + distance) % ring


def whole(shape):
    return pl.BlockSpec(shape, lambda i: (0,) * len(shape))


def pack_kernel(q_ref, w_ref, qw_ref):
    heads, rows, size = q_ref.shape
    for h in range(heads):
        qw_ref[h * rows : (h + 1) * rows] = q_ref[h]
    w_heads, deep, wide = w_ref.shape
    group, tiles = 16 // deep, wide // 128
    for g in range(w_heads // group):
        lines = jnp.concatenate([w_ref[g * group + k].astype(jnp.float32) for k in range(group)], axis=0)
        lines = lines.astype(jnp.bfloat16)
        for t in range(tiles):
            at = heads * rows + (g * tiles + t) * 16
            qw_ref[at : at + 16] = lines[:, t * 128 : (t + 1) * 128]


def pack(q, w):
    heads, rows, size = q.shape
    lines = heads * rows + math.prod(w.shape) // 128
    return pl.pallas_call(
        pack_kernel,
        out_shape=jax.ShapeDtypeStruct((lines, 128), jnp.bfloat16),
        grid=(1,),
        in_specs=[whole(q.shape), whole(w.shape)],
        out_specs=whole((lines, 128)),
        compiler_params=ROOMY,
        name="pack",
    )(q, w)


def unpack_kernel(heads, rows, deep, idx_ref, own_ref, far_ref, query_ref, w_ref):
    first = idx_ref[1] == 0
    w_heads, _, wide = w_ref.shape
    turn = jnp.where(idx_ref[2] == 0, w_heads // 2, 0)

    def lines(at, count):
        near = [own_ref[core, at : at + count] for core in range(2)]
        far = [far_ref[core, at : at + count] for core in range(2)]
        low = [jnp.where(first, a, b) for a, b in zip(near, far)]
        return low + [jnp.where(first, b, a) for a, b in zip(near, far)]

    for h in range(heads):
        for block, value in enumerate(lines(h * rows, rows)):
            query_ref[h, block * rows : (block + 1) * rows] = value
    group, tiles = 16 // deep, wide // 128
    for g in range(w_heads // group):
        for t in range(tiles):
            tile = [x.astype(jnp.float32) for x in lines(heads * rows + (g * tiles + t) * 16, 16)]
            for k in range(group):
                piece = jnp.concatenate([x[k * deep : (k + 1) * deep] for x in tile], axis=0).astype(jnp.bfloat16)
                w_ref[(g * group + k + turn) % w_heads, :, t * 128 : (t + 1) * 128] = piece


def unpack(idx, own, far, heads, rows, w_shape):
    w_heads, deep, wide = w_shape
    return pl.pallas_call(
        functools.partial(unpack_kernel, heads, rows, deep),
        out_shape=(
            jax.ShapeDtypeStruct((heads, 4 * rows, 128), jnp.bfloat16),
            jax.ShapeDtypeStruct((w_heads, 4 * deep, wide), jnp.bfloat16),
        ),
        in_specs=[SMEM, VMEM, VMEM],
        out_specs=(VMEM, VMEM),
        compiler_params=PARAMS,
        cost_estimate=pl.CostEstimate(flops=1 << 28, bytes_accessed=1 << 20, transcendentals=0),
        name="unpack",
    )(idx, own, far)


def near_kernel(rows, heads, ring, scale2, idx_ref, q_ref, own_ref, b1_ref, b2_ref, m_ref, l_ref, acc_ref):
    y, zh, c = idx_ref[0], idx_ref[1], idx_ref[2]
    query_pos = lax.broadcasted_iota(jnp.int32, (1, 4 * rows), 1)
    key_pos = (zh * 2 + c) * rows + lax.broadcasted_iota(jnp.int32, (rows, 1), 0)
    own_seen = query_pos >= (zh * 2 + c) * rows
    for h in range(heads):
        query = q_ref[h]
        state = attend_block(
            None, scale2, query, own_ref[0, h], own_ref[1, h], own_seen, key_pos <= query_pos
        )
        for distance, block_ref in ((1, b1_ref), (2, b2_ref)):
            seen = source_of(idx_ref, ring, distance) < y
            state = attend_block(state, scale2, query, *chip_block(block_ref, h), seen)
        m_ref[h], l_ref[h], acc_ref[h] = state


def far_kernel(rows, heads, ring, scale2, idx_ref, q_ref, b3_ref, b4_ref, m_ref, l_ref, acc_ref, keep_ref, send_ref):
    y, zh, c = idx_ref[0], idx_ref[1], idx_ref[2]

    def put(z, at, first, second):
        place = jnp.where(zh == z, 0, 1)
        keep_ref[place, at : at + first.shape[0]] = jnp.where(c == 0, first, second)
        send_ref[place, at : at + first.shape[0]] = jnp.where(c == 0, second, first)

    line = lax.broadcasted_iota(jnp.int32, (16, 4 * rows), 0)
    plane = jnp.zeros((16, 4 * rows), jnp.float32)
    for h in range(heads):
        query = q_ref[h]
        state = m_ref[h], l_ref[h], acc_ref[h]
        seen = source_of(idx_ref, ring, 4) < y
        state = attend_block(state, scale2, query, b4_ref[0, h], b4_ref[1, h], seen)
        seen = source_of(idx_ref, ring, 3) < y
        most, total, sums = attend_block(state, scale2, query, *chip_block(b3_ref, h), seen)
        seen = total > 0.0
        safe = jnp.where(seen, total, 1.0)
        low = jnp.transpose(sums * (1.0 / safe)).astype(jnp.bfloat16)
        for z in range(2):
            put(z, h * rows, low[2 * z * rows : (2 * z + 1) * rows], low[(2 * z + 1) * rows : (2 * z + 2) * rows])
        log = jnp.where(seen, most + jnp.log2(safe), LOW)
        for part, piece in enumerate(split3(log)):
            plane = jnp.where(line == 3 * h + part, piece, plane)
    plane = jnp.concatenate([plane, jnp.zeros((16, 128), jnp.float32)], axis=1)
    for z in range(2):
        first, second = [
            plane[:, block * rows : block * rows + 256].astype(jnp.bfloat16) for block in (2 * z, 2 * z + 1)
        ]
        put(z, heads * rows, first[:, :128], second[:, :128])
        put(z, heads * rows + 16, first[:, 128:], second[:, 128:])


def state_shapes(heads, rows, size, kind):
    return (
        kind((heads, 1, 4 * rows), jnp.float32),
        kind((heads, 1, 4 * rows), jnp.float32),
        kind((heads, size, 4 * rows), jnp.float32),
    )


def attend_near(idx, query, own, b1, b2, ring):
    heads, rows, size = query.shape[0], query.shape[1] // 4, query.shape[2]
    scale2 = size ** (-0.5) * math.log2(math.e)
    keys = 5 * rows
    return pl.pallas_call(
        functools.partial(near_kernel, rows, heads, ring, scale2),
        out_shape=state_shapes(heads, rows, size, jax.ShapeDtypeStruct),
        in_specs=[SMEM] + [VMEM] * 4,
        out_specs=(VMEM,) * 3,
        compiler_params=PARAMS,
        cost_estimate=pl.CostEstimate(flops=1 << 28, bytes_accessed=1 << 18, transcendentals=0),
        name="attend_near",
    )(idx, query, own, b1, b2)


def attend_far(idx, query, b3, b4, state, ring):
    heads, rows, size = query.shape[0], query.shape[1] // 4, query.shape[2]
    scale2 = size ** (-0.5) * math.log2(math.e)
    out = jax.ShapeDtypeStruct((2, heads * rows + 32, size), jnp.bfloat16)
    keys = 3 * rows
    return pl.pallas_call(
        functools.partial(far_kernel, rows, heads, ring, scale2),
        out_shape=(out, out),
        in_specs=[SMEM] + [VMEM] * 6,
        out_specs=(VMEM, VMEM),
        compiler_params=PARAMS,
        cost_estimate=pl.CostEstimate(flops=1 << 31, bytes_accessed=1 << 18, transcendentals=0),
        name="attend_far",
    )(idx, query, b3, b4, *state)


def merge_two(rows, heads, a, b, out_ref, last):
    at = heads * rows
    planes = [jnp.concatenate([x[at : at + 16], x[at + 16 : at + 32]], axis=1).astype(jnp.float32) for x in (a, b)]
    line = lax.broadcasted_iota(jnp.int32, (128, 256), 0)
    shares = jnp.zeros((128, 256), jnp.float32)
    logs = jnp.zeros((16, 256), jnp.float32)
    for h in range(heads):
        log_a, log_b = [p[3 * h : 3 * h + 1] + p[3 * h + 1 : 3 * h + 2] + p[3 * h + 2 : 3 * h + 3] for p in planes]
        top = jnp.maximum(log_a, log_b)
        part_a, part_b = jnp.exp2(log_a - top), jnp.exp2(log_b - top)
        total = part_a + part_b
        shares = jnp.where(line == 2 * h, part_a / total, shares)
        shares = jnp.where(line == 2 * h + 1, part_b / total, shares)
        for part, piece in enumerate(split3(top + jnp.log2(total))):
            logs = jnp.where(line[:16] == 3 * h + part, piece, logs)
    shares = jnp.transpose(shares)[:rows]
    for h in range(heads):
        value = a[h * rows : (h + 1) * rows].astype(jnp.float32) * shares[:, 2 * h : 2 * h + 1]
        value = value + b[h * rows : (h + 1) * rows].astype(jnp.float32) * shares[:, 2 * h + 1 : 2 * h + 2]
        out_ref[h * rows : (h + 1) * rows] = value.astype(jnp.bfloat16)
    if not last:
        low = logs.astype(jnp.bfloat16)
        out_ref[at : at + 16] = low[:, :128]
        out_ref[at + 16 : at + 32] = low[:, 128:]


def merge_core_kernel(rows, heads, idx_ref, a_ref, b_ref, keep_ref, send_ref):
    other = 1 - idx_ref[2]
    merge_two(rows, heads, a_ref[1], b_ref[other, 1], send_ref, False)
    merge_two(rows, heads, a_ref[0], b_ref[other, 0], keep_ref, False)


def merge_far_kernel(rows, heads, a_ref, b_ref, out_ref):
    merge_two(rows, heads, a_ref[...], b_ref[...], out_ref, True)


def merge_core(idx, keep, both, heads):
    _, lines, size = keep.shape
    out = jax.ShapeDtypeStruct((lines, size), jnp.bfloat16)
    return pl.pallas_call(
        functools.partial(merge_core_kernel, (lines - 32) // heads, heads),
        out_shape=(out, out),
        in_specs=[SMEM, VMEM, VMEM],
        out_specs=(VMEM, VMEM),
        compiler_params=PARAMS,
        name="merge_core",
    )(idx, keep, both)


def merge_far(keep, other, heads):
    lines, size = keep.shape
    return pl.pallas_call(
        functools.partial(merge_far_kernel, (lines - 32) // heads, heads),
        out_shape=jax.ShapeDtypeStruct((lines - 32, size), jnp.bfloat16),
        in_specs=[VMEM, VMEM],
        out_specs=VMEM,
        compiler_params=PARAMS,
        cost_estimate=pl.CostEstimate(flops=1 << 31, bytes_accessed=7 << 20, transcendentals=0),
        name="merge_far",
    )(keep, other)


def project_kernel(ring, idx_ref, att_ref, w0_ref, w1_ref, w2_ref, w3_ref, w4_ref, keep_ref, send_ref):
    y, c = idx_ref[0], idx_ref[2]
    cores, heads, rows, size = att_ref.shape
    deep = w0_ref.shape[1]
    line = lax.broadcasted_iota(jnp.int32, (size, size), 0)
    lane = lax.broadcasted_iota(jnp.int32, (size, size), 1)
    sources = [jnp.where(c == 0, (y + ring - hops) % ring, (y + hops) % ring) for hops in (1, 2, 3)]
    lefts, rights = [], []
    for h in range(0, heads, 2):
        opposite = h < heads // 2
        if h % (heads // 2) == 0:
            moves = []
            for side in range(2):
                wanted = jnp.full((size, size), -1, jnp.int32)
                for slot, source in enumerate([(y + 4) % ring if opposite else y] + sources):
                    at = side * size // 2 + slot * deep
                    inside = jnp.logical_and(lane >= at, lane < at + deep)
                    wanted = jnp.where(inside, lane + (source * deep - at), wanted)
                moves.append(jnp.where(line == wanted, 1.0, 0.0).astype(jnp.bfloat16))
        left = None
        for side in range(2):
            place = (h + side + jnp.where(c == 0, heads // 2, 0)) % heads
            columns = jnp.concatenate([att_ref[core, place] for core in range(cores)], axis=0)
            moved = jnp.dot(columns, moves[side], preferred_element_type=jnp.float32)
            left = moved if left is None else left + moved
            rights += [(ref, h + side) for ref in (w4_ref if opposite else w0_ref, w1_ref, w2_ref, w3_ref)]
        lefts.append(left.astype(jnp.bfloat16))
    left = jnp.concatenate(lefts, axis=1)
    for at in range(0, w0_ref.shape[2], 256):
        right = jnp.concatenate([ref[h, :, at : at + 256] for ref, h in rights], axis=0)
        total = jnp.dot(left, right, preferred_element_type=jnp.float32)
        first, second = total[:rows], total[rows:]
        keep_ref[:, at : at + 256] = jnp.where(c == 0, first, second)
        send_ref[:, at : at + 256] = jnp.where(c == 0, second, first).astype(jnp.bfloat16)


def project(idx, attended, weights, ring):
    _, _, rows, _ = attended.shape
    shape = (rows, weights[0].shape[2])
    return pl.pallas_call(
        functools.partial(project_kernel, ring),
        out_shape=(jax.ShapeDtypeStruct(shape, jnp.float32), jax.ShapeDtypeStruct(shape, jnp.bfloat16)),
        in_specs=[SMEM] + [VMEM] * (1 + len(weights)),
        out_specs=(VMEM, VMEM),
        compiler_params=PARAMS,
        name="project",
    )(idx, attended, *weights)


def join_kernel(idx_ref, keep_ref, other_ref, out_ref):
    out_ref[...] = (keep_ref[...] + other_ref[0].astype(jnp.float32)).astype(jnp.bfloat16)


def join(idx, keep, both):
    _, rows, wide = both.shape
    half = wide // 2
    mine = pl.BlockSpec((rows, half), lambda i, idx_ref: (0, i))
    return pl.pallas_call(
        join_kernel,
        out_shape=jax.ShapeDtypeStruct((rows, wide), jnp.bfloat16),
        grid_spec=pltpu.PrefetchScalarGridSpec(
            num_scalar_prefetch=1,
            grid=(2,),
            in_specs=[mine, pl.BlockSpec((1, rows, half), lambda i, idx_ref: (1 - idx_ref[2], 0, i))],
            out_specs=mine,
        ),
        compiler_params=PARAMS,
        name="join",
    )(idx, keep, both)


def finish_kernel(pieces_ref, bias_ref, out_ref):
    total = pieces_ref[0].astype(jnp.float32)
    for part in range(1, pieces_ref.shape[0]):
        total = total + pieces_ref[part].astype(jnp.float32)
    out_ref[...] = (total + bias_ref[...]).astype(jnp.bfloat16)


def finish(pieces, bias):
    return pl.pallas_call(
        finish_kernel,
        out_shape=jax.ShapeDtypeStruct(pieces.shape[1:], jnp.bfloat16),
        in_specs=[VMEM, VMEM],
        out_specs=VMEM,
        compiler_params=PARAMS,
        name="finish",
    )(pieces, bias)


def on_device(query_rows, key_rows, value_rows, out_weight, out_bias):
    rows, heads, size = query_rows.shape
    ring = lax.axis_size("y")
    y, zh, c = lax.axis_index("y"), lax.axis_index("zh"), lax.axis_index("c")
    idx = jnp.stack([y, zh, c]).astype(jnp.int32)

    def onward(block, hops):
        pairs = []
        for at in range(ring):
            pairs.append((2 * at, 2 * ((at + hops) % ring)))
            pairs.append((2 * at + 1, 2 * ((at - hops) % ring) + 1))
        return lax.ppermute(block, ("y", "c"), pairs)

    swap = [(0, 1), (1, 0)]

    own = jnp.stack([jnp.swapaxes(key_rows, 0, 1), jnp.swapaxes(value_rows, 0, 1)])
    chip = lax.all_gather(own, "c", axis=0)
    b2 = onward(chip, 2)
    query, weight, _ = lax.optimization_barrier((jnp.swapaxes(query_rows, 0, 1), out_weight, chip))
    qw = pack(query, weight)
    near_chip, qw = lax.optimization_barrier((chip, qw))
    b1 = onward(near_chip, 1)
    qw_far = lax.ppermute(qw, "zh", swap)
    qw_own = lax.all_gather(qw, "c", axis=0)
    qw_far = lax.all_gather(qw_far, "c", axis=0)
    b2, qw_own = lax.optimization_barrier((b2, qw_own))
    b3 = onward(b2, 1)
    b4 = onward(lax.dynamic_index_in_dim(b2, c, 0, keepdims=False), 2)
    query, weight = unpack(idx, qw_own, qw_far, heads, rows, out_weight.shape)
    state = attend_near(idx, query, own, b1, b2, ring)

    weight, state = lax.optimization_barrier((weight, state))
    w2 = onward(weight, 2)
    w1 = onward(weight, 1)
    keep, send = attend_far(idx, query, b3, b4, state, ring)
    keep, send = merge_core(idx, keep, lax.all_gather(send, "c", axis=0), heads)
    other = lax.ppermute(send, "zh", swap)
    w3 = onward(w2, 1)
    w4 = onward(w2[: w2.shape[0] // 2], 2)
    attended = merge_far(keep, other, heads)
    attended = attended.reshape(heads, rows, size)
    attended = lax.all_gather(attended, "col", axis=0, tiled=True)
    attended = lax.all_gather(attended, "c", axis=0)
    keep, send = project(idx, attended, (weight, w1, w2, w3, w4), ring)
    joined = join(idx, keep, lax.all_gather(send, "c", axis=0))
    parts = lax.axis_size("row")
    pieces = joined.reshape(parts, rows // parts, joined.shape[1])
    pieces = lax.all_to_all(pieces, "row", 0, 0, tiled=True)
    return finish(pieces, out_bias[None, :])


def solution(mesh):
    shape = mesh.devices.shape
    fine = Mesh(mesh.devices.reshape((shape[0] // 4, 2, 2) + shape[1:]), ("y", "zh", "c", "row", "col"))
    seq = ("y", "zh", "c")
    in_specs = (
        P(seq, ("row", "col"), None),
        P(seq, ("row", "col"), None),
        P(seq, ("row", "col"), None),
        P("row", seq, "col"),
        P("col"),
    )
    out_specs = P(seq + ("row",), "col")
    return jax.shard_map(
        on_device, mesh=fine, in_specs=in_specs, out_specs=out_specs, check_vma=False
    )
```
